32 devices in a mesh: seq: 8 (over y, x, core), dp: 4 (over z).
Axes of the slice: x: 2, y: 2, z: 4, core: 2. Of those that a mesh axis runs over, the one named last changes fastest.
Arguments:
- tokens: bfloat16 [4096, 1024], P(('dp', 'seq')), parts along dimension 0, may hold values from -6 to 6
- norm_gain: float32 [1024], replicated, may hold values from 0.1 to 1.9
- filters: float32 [12, 1024], P(None, 'seq'), may hold values from -0.1875 to 0.1875
- mixing: bfloat16 [12, 1024, 1024], P(None, 'seq'), may hold values from -0.0546875 to 0.0546875
Outputs:
- mixed: bfloat16 [4096, 1024], P(('dp', 'seq')), parts along dimension 0
The draws below stay inside these ranges and needn't reach their ends.
There are 4 independent parts, one for each index of `dp`. The reference program is written for one: setup_inputs(seed, part) draws one part's arguments, and reference() takes and returns one part's arrays. A program takes and returns all parts, laid end to end along the dimension named above; an argument that names none is the same for every part. Nothing has to cross between parts.
All inputs are finite; a program needn't handle non-finite values.
Results may differ from the reference program's by a relative error of at most 0.0044.
Values may be sent and summed in bfloat16 or wider, within the bound.
No kernel may reach another device: no remote copies, remote signals or barrier semaphores. Data moves between devices by JAX's collectives and lax.ppermute only.
A program may use at most 192 MiB of HBM per device.

```python
import jax
import jax.numpy as jnp
from jax import lax

D = 1024
K = 12
LENGTH = 1024


def block_levels(stream_key, dims, shards, least, high):
    def one(axis_at, parts):
        draws = jax.random.uniform(jax.random.fold_in(jax.random.fold_in(stream_key, 6), axis_at), (parts,), jnp.float32, least / len(shards), high / len(shards))
        return jnp.repeat(jnp.exp(draws), dims[axis_at] // parts).reshape((-1,) + (1,) * (len(dims) - axis_at - 1))

    gain = one(*shards[0])
    for cut in shards[1:]:
        gain = gain * one(*cut)
    return gain


def gaussian(key, dims, width, limit, shards=(), dtype=jnp.bfloat16):
    entries = jax.random.normal(key, dims, jnp.float32) * width
    if len(shards) > 0:
        entries = block_levels(key, dims, shards, -0.22, 0.18) * entries
    return jnp.clip(entries, min=-limit, max=limit).astype(dtype)


def setup_inputs(seed: int = 0, part: int = 0) -> dict:
    keys = jax.random.split(jax.random.key(seed), 5)
    part_splits = jax.random.split(jax.random.fold_in(keys[4], part), 5)
    tokens = gaussian(part_splits[0], (LENGTH, D), 1.0, 6.0, ((0, 8),))
    norm_gain = jnp.clip(1.0 + 0.18 * jax.random.normal(keys[1], (D,), jnp.float32), 0.1, 1.9)
    filters = gaussian(keys[2], (K, LENGTH), LENGTH ** -0.5, 0.1875, ((1, 8),), jnp.float32)
    mixing = gaussian(keys[3], (K, D, D), (K * D) ** -0.5, 0.0546875, ((1, 8),))
    return {"tokens": tokens, "norm_gain": norm_gain, "filters": filters, "mixing": mixing}


def reference(tokens, norm_gain, filters, mixing):
    values = tokens.astype(jnp.float32)
    scale_row = lax.rsqrt(lax.optimization_barrier(jnp.mean(values * values, axis=1, keepdims=True)) + 1e-05)
    normed = (values * scale_row * norm_gain).astype(jnp.bfloat16)
    total = 2 * LENGTH
    signal_hat = jnp.fft.rfft(normed.astype(jnp.float32), n=total, axis=0)
    filter_hat = jnp.fft.rfft(filters, n=total, axis=1)

    def one_filter(carry, inputs):
        spectrum, weight = inputs
        conv = jnp.fft.irfft(signal_hat * spectrum[:, None], n=total, axis=0)[:LENGTH]
        feats = conv.astype(jnp.bfloat16)
        return (carry + jnp.dot(feats, weight, preferred_element_type=jnp.float32), None)
    start = jnp.zeros((LENGTH, D), jnp.float32)
    branch, unused = lax.scan(one_filter, start, (filter_hat, mixing))
    return (values + branch).astype(jnp.bfloat16)
```

```python
import functools

import jax
import jax.numpy as jnp
from jax import lax
from jax.experimental import pallas as pl
from jax.experimental.pallas import tpu as pltpu
from jax.sharding import PartitionSpec as P

MIB = 1024 * 1024
EXTRA = 16
VMEM = pl.BlockSpec(memory_space=pltpu.VMEM)
SMEM = pl.BlockSpec(memory_space=pltpu.SMEM)
HBM = pl.BlockSpec(memory_space=pltpu.HBM)


def swap(value, bits, size):
    return lax.ppermute(value, "seq", [(i, i ^ bits) for i in range(size)])


def kernel_call(kernel, name, out_shape, specs, limit, scratch=()):
    return pl.pallas_call(
        kernel,
        out_shape=out_shape,
        in_specs=specs,
        out_specs=jax.tree.map(lambda _: VMEM, out_shape),
        scratch_shapes=scratch,
        compiler_params=pltpu.CompilerParams(vmem_limit_bytes=limit),
        name=name,
    )


def in_hbm(value):
    return pltpu.with_memory_space_constraint(value, pltpu.HBM)


def norm_kernel(tokens_hbm, gain_hbm, filters_hbm, *refs):
    *out_refs, tokens_ref, gain_ref, filters_ref, sems = refs
    pairs = ((filters_hbm, filters_ref), (gain_hbm, gain_ref), (tokens_hbm, tokens_ref))
    copies = [pltpu.make_async_copy(a, b, sems.at[i]) for i, (a, b) in enumerate(pairs)]
    for copy in copies:
        copy.start()
    chip = lax.axis_index("seq") // 2
    rows, width = tokens_ref.shape
    chips = len(out_refs)
    count = width // chips
    num, span = filters_ref.shape
    packed = out_refs[0].shape[0] > rows
    copies[0].wait()
    if packed:
        flip = (
            lax.broadcasted_iota(jnp.int32, (span, span), 0)
            + lax.broadcasted_iota(jnp.int32, (span, span), 1)
            == span - 1
        ).astype(jnp.bfloat16)
        taps = jnp.dot(
            filters_ref[...].astype(jnp.bfloat16), flip, preferred_element_type=jnp.float32
        )
        taps = jnp.concatenate([taps, jnp.zeros((EXTRA - num, span), jnp.float32)], axis=0)
        taps = jnp.concatenate([taps, jnp.zeros((EXTRA, count - span), jnp.float32)], axis=1)
        taps = taps.astype(jnp.bfloat16)
    copies[1].wait()
    copies[2].wait()
    values = tokens_ref[...].astype(jnp.float32)
    scale = lax.rsqrt(jnp.mean(values * values, axis=1, keepdims=True) + 1e-05)
    normed = (values * scale * gain_ref[...]).astype(jnp.bfloat16)
    for part in range(chips):
        for shift, out_ref in enumerate(out_refs):

            @pl.when(chip == part ^ shift)
            def _(part=part, out_ref=out_ref):
                out_ref[0:rows, :] = normed[:, part * count : (part + 1) * count]

    if packed:
        for out_ref in out_refs:
            out_ref[rows:, :] = taps


def strip_kernel(chips, rows, num, packed, *refs):
    own = refs[:chips]
    pair = refs[chips : 2 * chips]
    refs = refs[2 * chips :]
    mix_hbm, *refs = refs
    if not packed:
        taps_ref, *refs = refs
    signal, strip, mix_ref, base, sem = refs
    copy = pltpu.make_async_copy(mix_hbm, mix_ref, sem)
    copy.start()
    index = lax.axis_index("seq")
    chip = index // 2
    core = index % 2
    devices = 2 * chips
    length = devices * rows
    half = signal.shape[1] // 2
    wide = length + 2 * rows
    base[:, length:] = jnp.zeros((base.shape[0], 2 * rows), jnp.float32)
    for shift in range(chips):
        for which, block in enumerate((own[shift], pair[shift])):
            place = 2 * (chip ^ shift) + (core if which == 0 else 1 - core)
            value = block[0:rows, :]
            turned = jnp.concatenate([value[:, half:], value[:, :half]], axis=1)
            value = jnp.where(core == 0, value, turned)
            signal[pl.ds(pl.multiple_of(place * rows, rows), rows), :] = value
            if packed:
                at = pl.multiple_of((devices - 1 - place) * rows, rows)
                base[:, pl.ds(at, rows)] = block[rows:, 0:rows].astype(jnp.float32)
    if not packed:
        base[:, 0:length] = taps_ref[...]

    def one_filter(k, carry):
        line = jnp.broadcast_to(base[pl.ds(k, 1), :], (8, wide))
        line = pltpu.roll(line, wide - rows + 1, 1, stride=1, stride_axis=0)
        for step in range(rows // 16):
            pieces = [pltpu.roll(line, 16 * step + 8 * h, 1)[:, : length + rows] for h in (0, 1)]
            at = pl.multiple_of(k * rows + 16 * step, 16)
            strip[pl.ds(at, 16), :] = jnp.concatenate(pieces, axis=0).astype(jnp.bfloat16)
        return carry

    lax.fori_loop(0, num, one_filter, 0, unroll=3 if packed else 1)
    copy.wait()


def branch_kernel(chips, rows, shift, *refs):
    if shift is None:
        shift_ref, *refs = refs
        shift = shift_ref[0]
    signal, strip, mix_ref, pair_mix_ref, out_ref, feats = refs
    index = lax.axis_index("seq")
    core = index % 2
    other = (index // 2) ^ shift
    devices = 2 * chips
    num, half, width = mix_ref.shape
    count = 2 * half
    offset = (devices - 1 - (2 * other + core)) * rows
    if chips <= 4:

        def convolve(steps):
            depth = 2 * rows * steps
            left = strip[:, pl.ds(pl.multiple_of(offset, rows), depth)]
            total = jnp.dot(left, signal[0:depth, :], preferred_element_type=jnp.float32)
            for k in range(num):
                for which in range(2):
                    at = (which * num + k) * half
                    feats[:, at : at + half] = total[
                        k * rows : (k + 1) * rows, which * half : (which + 1) * half
                    ].astype(jnp.bfloat16)

        for steps in range(1, chips + 1):
            pl.when(other == steps - 1)(functools.partial(convolve, steps))
        both = num * half
        total = jnp.dot(
            feats[:, :both],
            mix_ref[...].reshape(both, width),
            preferred_element_type=jnp.float32,
        ) + jnp.dot(
            feats[:, both:],
            pair_mix_ref[...].reshape(both, width),
            preferred_element_type=jnp.float32,
        )
    else:
        feats[...] = jnp.zeros(feats.shape, jnp.float32)

        def add_tokens(step, carry):
            at = pl.multiple_of(2 * rows * step, 2 * rows)
            left = strip[:, pl.ds(pl.multiple_of(offset + at, rows), 2 * rows)]
            feats[...] += jnp.dot(
                left, signal[pl.ds(at, 2 * rows), :], preferred_element_type=jnp.float32
            )
            return carry

        lax.fori_loop(0, other + 1, add_tokens, 0)
        total = jnp.zeros((rows, width), jnp.float32)
        for k in range(num):
            found = feats[k * rows : (k + 1) * rows, :].astype(jnp.bfloat16)
            weight = jnp.concatenate([mix_ref[k], pair_mix_ref[k]], axis=0)
            total += jnp.dot(found, weight, preferred_element_type=jnp.float32)
    out_ref[...] = total.astype(out_ref.dtype)


def local(tokens, norm_gain, filters, mixing):
    rows, width = tokens.shape
    devices = lax.axis_size("seq")
    chips = devices // 2
    num, span = filters.shape
    length = devices * rows
    count = width // chips
    packed = count >= span
    few = chips <= 4
    pair_mixing = swap(mixing, 1, devices)
    tall = rows + (EXTRA if packed else 0)
    blocks = kernel_call(
        norm_kernel,
        "norm",
        [jax.ShapeDtypeStruct((tall, count), jnp.bfloat16)] * chips,
        [HBM] * 3,
        8 * MIB,
        [
            pltpu.VMEM((rows, width), tokens.dtype),
            pltpu.VMEM((1, width), norm_gain.dtype),
            pltpu.VMEM((num, span), filters.dtype),
            pltpu.SemaphoreType.DMA((3,)),
        ],
    )(in_hbm(tokens), in_hbm(norm_gain.reshape(1, width)), in_hbm(filters))
    far = [swap(blocks[s], 2 * s, devices) for s in reversed(range(1, chips))]
    own = [blocks[0], *reversed(far)]
    pair = [swap(block, 1, devices) for block in own]
    operands = [*own, *pair, in_hbm(mixing)]
    specs = [VMEM] * (2 * chips) + [HBM]
    if not packed:
        taps = lax.all_gather(filters, "seq", axis=1, tiled=True)[:, ::-1]
        operands.append(jnp.pad(taps, ((0, EXTRA - num), (0, 0))))
        specs.append(VMEM)
    signal, strip, near_mixing = kernel_call(
        functools.partial(strip_kernel, chips, rows, num, packed),
        "strip",
        [
            jax.ShapeDtypeStruct((length, count), jnp.bfloat16),
            jax.ShapeDtypeStruct((num * rows, length + rows), jnp.bfloat16),
            jax.ShapeDtypeStruct(mixing.shape, mixing.dtype),
        ],
        specs,
        16 * MIB if few else 48 * MIB,
        [pltpu.VMEM((EXTRA, length + 2 * rows), jnp.float32), pltpu.SemaphoreType.DMA(())],
    )(*operands)
    fixed = [signal, strip, near_mixing, pair_mixing]
    if few:

        def branch(shift, dtype):
            return kernel_call(
                functools.partial(branch_kernel, chips, rows, shift),
                "branch",
                jax.ShapeDtypeStruct((rows, width), dtype),
                [VMEM] * 4,
                24 * MIB,
                [pltpu.VMEM((rows, num * count), jnp.bfloat16)],
            )(*fixed)

        parts = {s: branch(s, jnp.bfloat16) for s in reversed(range(1, chips))}
        total = branch(0, jnp.float32)
    else:

        def branch(shift):
            return kernel_call(
                functools.partial(branch_kernel, chips, rows, None),
                "branch",
                jax.ShapeDtypeStruct((rows, width), jnp.bfloat16),
                [SMEM] + [VMEM] * 4,
                48 * MIB,
                [pltpu.VMEM((num * rows, count), jnp.float32)],
            )(shift.reshape(1), *fixed)

        parts = lax.map(branch, jnp.arange(chips, dtype=jnp.int32))
        total = parts[0].astype(jnp.float32)
        parts = {s: parts[s] for s in range(1, chips)}
    sent = [swap(value, 2 * s, devices) for s, value in parts.items()]
    total = tokens.astype(jnp.float32) + total
    for value in sent:
        total = total + value.astype(jnp.float32)
    return total.astype(jnp.bfloat16)


def solution(mesh):
    in_specs = (P(("dp", "seq"), None), P(), P(None, "seq"), P(None, "seq", None))
    out_specs = P(("dp", "seq"), None)
    return jax.shard_map(local, mesh=mesh, in_specs=in_specs, out_specs=out_specs, check_vma=False)
```

```python
import functools

import jax
import jax.numpy as jnp
from jax import lax
from jax.experimental import pallas as pl
from jax.experimental.pallas import tpu as pltpu
from jax.sharding import PartitionSpec as P

MIB = 1024 * 1024
EXTRA = 16
VMEM = pl.BlockSpec(memory_space=pltpu.VMEM)
SMEM = pl.BlockSpec(memory_space=pltpu.SMEM)
HBM = pl.BlockSpec(memory_space=pltpu.HBM)


def swap(value, bits, size):
    return lax.ppermute(value, "seq", [(i, i ^ bits) for i in range(size)])


def kernel_call(kernel, name, out_shape, specs, limit, scratch=()):
    return pl.pallas_call(
        kernel,
        out_shape=out_shape,
        in_specs=specs,
        out_specs=jax.tree.map(lambda _: VMEM, out_shape),
        scratch_shapes=scratch,
        compiler_params=pltpu.CompilerParams(vmem_limit_bytes=limit),
        name=name,
    )


def in_hbm(value):
    return pltpu.with_memory_space_constraint(value, pltpu.HBM)


def norm_kernel(tokens_hbm, gain_hbm, filters_hbm, *refs):
    *out_refs, tokens_ref, gain_ref, filters_ref, sems = refs
    pairs = ((filters_hbm, filters_ref), (gain_hbm, gain_ref), (tokens_hbm, tokens_ref))
    copies = [pltpu.make_async_copy(a, b, sems.at[i]) for i, (a, b) in enumerate(pairs)]
    for copy in copies:
        copy.start()
    chip = lax.axis_index("seq") // 2
    rows, width = tokens_ref.shape
    chips = len(out_refs)
    count = width // chips
    num, span = filters_ref.shape
    packed = out_refs[0].shape[0] > rows
    copies[0].wait()
    if packed:
        flip = (
            lax.broadcasted_iota(jnp.int32, (span, span), 0)
            + lax.broadcasted_iota(jnp.int32, (span, span), 1)
            == span - 1
        ).astype(jnp.bfloat16)
        taps = jnp.dot(
            filters_ref[...].astype(jnp.bfloat16), flip, preferred_element_type=jnp.float32
        )
        taps = jnp.concatenate([taps, jnp.zeros((EXTRA - num, span), jnp.float32)], axis=0)
        taps = jnp.concatenate([taps, jnp.zeros((EXTRA, count - span), jnp.float32)], axis=1)
        taps = taps.astype(jnp.bfloat16)
    copies[1].wait()
    copies[2].wait()
    values = tokens_ref[...].astype(jnp.float32)
    scale = lax.rsqrt(jnp.mean(values * values, axis=1, keepdims=True) + 1e-05)
    normed = (values * scale * gain_ref[...]).astype(jnp.bfloat16)
    for part in range(chips):
        for shift, out_ref in enumerate(out_refs):

            @pl.when(chip == part ^ shift)
            def _(part=part, out_ref=out_ref):
                out_ref[0:rows, :] = normed[:, part * count : (part + 1) * count]

    if packed:
        for out_ref in out_refs:
            out_ref[rows:, :] = taps


def aim(chip, core, kind):
    if kind == "far":
        return chip ^ 3, 1 - core
    if kind == "own":
        return chip, core
    return chip ^ (1 + core), core if kind == "same" else 1 - core


def write_features(feats, total, k, half, num):
    for which in range(2):
        at = (which * num + k) * half
        feats[:, at : at + half] = total[:, which * half : (which + 1) * half].astype(jnp.bfloat16)


def project(feats, mix_ref, pair_mix_ref):
    num, half, width = mix_ref.shape
    both = num * half
    return jnp.dot(
        feats[:, :both],
        mix_ref[...].reshape(both, width),
        preferred_element_type=jnp.float32,
    ) + jnp.dot(
        feats[:, both:],
        pair_mix_ref[...].reshape(both, width),
        preferred_element_type=jnp.float32,
    )


def strip_kernel(chips, rows, num, packed, *refs):
    own = refs[:chips]
    pair = refs[chips : 2 * chips]
    mix_hbm, *refs = refs[2 * chips :]
    if not packed:
        taps_ref, *refs = refs
    signal, strip, mix_ref, base, sem = refs
    copy = pltpu.make_async_copy(mix_hbm, mix_ref, sem)
    copy.start()
    index = lax.axis_index("seq")
    chip = index // 2
    core = index % 2
    devices = 2 * chips
    length = devices * rows
    half = signal.shape[1] // 2
    wide = length + 2 * rows
    base[:, length:] = jnp.zeros((base.shape[0], 2 * rows), jnp.float32)
    for shift in range(chips):
        for which, block in enumerate((own[shift], pair[shift])):
            place = 2 * (chip ^ shift) + (core if which == 0 else 1 - core)
            value = block[0:rows, :]
            turned = jnp.concatenate([value[:, half:], value[:, :half]], axis=1)
            value = jnp.where(core == 0, value, turned)
            signal[pl.ds(pl.multiple_of(place * rows, rows), rows), :] = value
            if packed:
                at = pl.multiple_of((devices - 1 - place) * rows, rows)
                base[:, pl.ds(at, rows)] = block[rows:, 0:rows].astype(jnp.float32)
    if not packed:
        base[:, 0:length] = taps_ref[...]

    def one_filter(k, carry):
        line = jnp.broadcast_to(base[pl.ds(k, 1), :], (8, wide))
        line = pltpu.roll(line, wide - rows + 1, 1, stride=1, stride_axis=0)
        for step in range(rows // 16):
            pieces = [pltpu.roll(line, 16 * step + 8 * h, 1)[:, : length + rows] for h in (0, 1)]
            at = pl.multiple_of(k * rows + 16 * step, 16)
            strip[pl.ds(at, 16), :] = jnp.concatenate(pieces, axis=0).astype(jnp.bfloat16)
        return carry

    lax.fori_loop(0, num, one_filter, 0, unroll=num if packed else 1)
    copy.wait()


def branch_kernel(chips, rows, kind, *refs):
    signal, strip, mix_ref, pair_mix_ref, out_ref, feats = refs
    index = lax.axis_index("seq")
    other, part = aim(index // 2, index % 2, kind)
    devices = 2 * chips
    num, half, width = mix_ref.shape
    offset = (devices - 1 - (2 * other + part)) * rows

    def convolve(steps):
        depth = 2 * rows * steps
        left = strip[:, pl.ds(pl.multiple_of(offset, rows), depth)]
        total = jnp.dot(left, signal[0:depth, :], preferred_element_type=jnp.float32)
        for k in range(num):
            write_features(feats, total[k * rows : (k + 1) * rows], k, half, num)

    for steps in range(1, chips + 1):
        pl.when(other == steps - 1)(functools.partial(convolve, steps))
    total = project(feats, mix_ref, pair_mix_ref)
    out_ref[...] = total.astype(out_ref.dtype)


def shifted_kernel(chips, rows, shift_ref, *refs):
    signal, strip, mix_ref, pair_mix_ref, out_ref, sums = refs
    index = lax.axis_index("seq")
    other = (index // 2) ^ shift_ref[0]
    devices = 2 * chips
    num, half, width = mix_ref.shape
    offset = (devices - 1 - (2 * other + index % 2)) * rows
    sums[...] = jnp.zeros(sums.shape, jnp.float32)

    def add_tokens(step, carry):
        at = pl.multiple_of(2 * rows * step, 2 * rows)
        left = strip[:, pl.ds(pl.multiple_of(offset + at, rows), 2 * rows)]
        sums[...] += jnp.dot(
            left, signal[pl.ds(at, 2 * rows), :], preferred_element_type=jnp.float32
        )
        return carry

    lax.fori_loop(0, other + 1, add_tokens, 0)
    total = jnp.zeros((rows, width), jnp.float32)
    for k in range(num):
        found = sums[k * rows : (k + 1) * rows, :].astype(jnp.bfloat16)
        weight = jnp.concatenate([mix_ref[k], pair_mix_ref[k]], axis=0)
        total += jnp.dot(found, weight, preferred_element_type=jnp.float32)
    out_ref[...] = total.astype(out_ref.dtype)


def local(tokens, norm_gain, filters, mixing):
    rows, width = tokens.shape
    devices = lax.axis_size("seq")
    chips = devices // 2
    num, span = filters.shape
    length = devices * rows
    count = width // chips
    packed = count >= span
    relay = chips == 4 and packed and count % 256 == 0
    pair_mixing = swap(mixing, 1, devices)
    tall = rows + (EXTRA if packed else 0)
    blocks = kernel_call(
        norm_kernel,
        "norm",
        [jax.ShapeDtypeStruct((tall, count), jnp.bfloat16)] * chips,
        [HBM] * 3,
        8 * MIB,
        [
            pltpu.VMEM((rows, width), tokens.dtype),
            pltpu.VMEM((1, width), norm_gain.dtype),
            pltpu.VMEM((num, span), filters.dtype),
            pltpu.SemaphoreType.DMA((3,)),
        ],
    )(in_hbm(tokens), in_hbm(norm_gain.reshape(1, width)), in_hbm(filters))
    far = [swap(blocks[s], 2 * s, devices) for s in reversed(range(1, chips))]
    own = [blocks[0], *reversed(far)]
    pair = [swap(block, 1, devices) for block in own]
    operands = [*own, *pair, in_hbm(mixing)]
    specs = [VMEM] * (2 * chips) + [HBM]
    feats = pltpu.VMEM((rows, num * count), jnp.bfloat16)
    shapes = [
        jax.ShapeDtypeStruct((length, count), jnp.bfloat16),
        jax.ShapeDtypeStruct((num * rows, length + rows), jnp.bfloat16),
        jax.ShapeDtypeStruct(mixing.shape, mixing.dtype),
    ]
    scratch = [
        pltpu.VMEM((EXTRA, length + 2 * rows), jnp.float32),
        pltpu.SemaphoreType.DMA(()),
    ]
    if not packed:
        taps = lax.all_gather(filters, "seq", axis=1, tiled=True)[:, ::-1]
        operands.append(jnp.pad(taps, ((0, EXTRA - num), (0, 0))))
        specs.append(VMEM)
    signal, strip, near_mixing = kernel_call(
        functools.partial(strip_kernel, chips, rows, num, packed),
        "strip",
        shapes,
        specs,
        24 * MIB if relay else 48 * MIB,
        scratch,
    )(*operands)
    fixed = [signal, strip, near_mixing, pair_mixing]
    total = tokens.astype(jnp.float32)
    if relay:

        def branch(kind, dtype):
            return kernel_call(
                functools.partial(branch_kernel, chips, rows, kind),
                "branch",
                jax.ShapeDtypeStruct((rows, width), dtype),
                [VMEM] * 4,
                24 * MIB,
                [feats],
            )(*fixed)

        pairs = [(c, q) for c in range(chips) for q in range(2)]
        across = [(2 * c + q, 2 * (c ^ (1 + q)) + 1 - q) for c, q in pairs]
        along = [(2 * c + q, 2 * (c ^ (1 + q)) + q) for c, q in pairs]
        far = lax.ppermute(branch("far", jnp.bfloat16), "seq", across)
        other = lax.ppermute(branch("other", jnp.bfloat16), "seq", across)
        same = (branch("same", jnp.float32) + far.astype(jnp.float32)).astype(jnp.bfloat16)
        same = lax.ppermute(same, "seq", along)
        total = total + branch("own", jnp.float32)
        sent = [other, same]
    else:

        def branch(shift):
            return kernel_call(
                functools.partial(shifted_kernel, chips, rows),
                "branch",
                jax.ShapeDtypeStruct((rows, width), jnp.bfloat16),
                [SMEM] + [VMEM] * 4,
                48 * MIB,
                [pltpu.VMEM((num * rows, count), jnp.float32)],
            )(shift.reshape(1), *fixed)

        parts = lax.map(branch, jnp.arange(chips, dtype=jnp.int32))
        sent = [parts[0]] + [swap(parts[s], 2 * s, devices) for s in range(1, chips)]
    for value in sent:
        total = total + value.astype(jnp.float32)
    return total.astype(jnp.bfloat16)


def solution(mesh):
    in_specs = (P(("dp", "seq"), None), P(), P(None, "seq"), P(None, "seq", None))
    out_specs = P(("dp", "seq"), None)
    return jax.shard_map(local, mesh=mesh, in_specs=in_specs, out_specs=out_specs, check_vma=False)
```

```python
import functools

import jax
import jax.numpy as jnp
from jax import lax
from jax.experimental import pallas as pl
from jax.experimental.pallas import tpu as pltpu
from jax.sharding import PartitionSpec as P

MIB = 1024 * 1024
EXTRA = 16
VMEM = pl.BlockSpec(memory_space=pltpu.VMEM)
SMEM = pl.BlockSpec(memory_space=pltpu.SMEM)
HBM = pl.BlockSpec(memory_space=pltpu.HBM)


def swap(value, bits, size):
    return lax.ppermute(value, "seq", [(i, i ^ bits) for i in range(size)])


def kernel_call(kernel, name, out_shape, specs, limit, scratch=()):
    return pl.pallas_call(
        kernel,
        out_shape=out_shape,
        in_specs=specs,
        out_specs=jax.tree.map(lambda _: VMEM, out_shape),
        scratch_shapes=scratch,
        compiler_params=pltpu.CompilerParams(vmem_limit_bytes=limit),
        name=name,
    )


def in_hbm(value):
    return pltpu.with_memory_space_constraint(value, pltpu.HBM)


def norm_kernel(tokens_hbm, gain_hbm, filters_hbm, *refs):
    *out_refs, tokens_ref, gain_ref, filters_ref, sems = refs
    pairs = ((filters_hbm, filters_ref), (gain_hbm, gain_ref), (tokens_hbm, tokens_ref))
    copies = [pltpu.make_async_copy(a, b, sems.at[i]) for i, (a, b) in enumerate(pairs)]
    for copy in copies:
        copy.start()
    chip = lax.axis_index("seq") // 2
    rows, width = tokens_ref.shape
    chips = len(out_refs)
    count = width // chips
    num, span = filters_ref.shape
    packed = out_refs[0].shape[0] > rows
    copies[0].wait()
    if packed:
        flip = (
            lax.broadcasted_iota(jnp.int32, (span, span), 0)
            + lax.broadcasted_iota(jnp.int32, (span, span), 1)
            == span - 1
        ).astype(jnp.bfloat16)
        taps = jnp.dot(
            filters_ref[...].astype(jnp.bfloat16), flip, preferred_element_type=jnp.float32
        )
        taps = jnp.concatenate([taps, jnp.zeros((EXTRA - num, span), jnp.float32)], axis=0)
        taps = jnp.concatenate([taps, jnp.zeros((EXTRA, count - span), jnp.float32)], axis=1)
        taps = taps.astype(jnp.bfloat16)
    copies[1].wait()
    copies[2].wait()
    values = tokens_ref[...].astype(jnp.float32)
    scale = lax.rsqrt(jnp.mean(values * values, axis=1, keepdims=True) + 1e-05)
    normed = (values * scale * gain_ref[...]).astype(jnp.bfloat16)
    for part in range(chips):
        for shift, out_ref in enumerate(out_refs):

            @pl.when(chip == part ^ shift)
            def _(part=part, out_ref=out_ref):
                out_ref[0:rows, :] = normed[:, part * count : (part + 1) * count]

    if packed:
        for out_ref in out_refs:
            out_ref[rows:, :] = taps


def stage_kernel(mix_hbm, block_ref, mix_ref, out_ref, sem):
    copy = pltpu.make_async_copy(mix_hbm, mix_ref, sem)
    copy.start()
    out_ref[...] = block_ref[...]
    copy.wait()


def aim(chip, core, kind):
    if kind == "far":
        return chip ^ 3, 1 - core
    if kind == "own":
        return chip, core
    return chip ^ (1 + core), core if kind == "same" else 1 - core


def project(feats, mix_ref, pair_mix_ref):
    num, half, width = mix_ref.shape
    both = num * half
    return jnp.dot(
        feats[:, :both],
        mix_ref[...].reshape(both, width),
        preferred_element_type=jnp.float32,
    ) + jnp.dot(
        feats[:, both:],
        pair_mix_ref[...].reshape(both, width),
        preferred_element_type=jnp.float32,
    )


def strip_kernel(chips, rows, num, fine, packed, *refs):
    own = refs[:chips]
    pair = refs[chips : 2 * chips]
    refs = refs[2 * chips :]
    if not packed:
        taps_ref, *refs = refs
    signal, strip, base = refs
    index = lax.axis_index("seq")
    chip = index // 2
    core = index % 2
    devices = 2 * chips
    length = devices * rows
    groups = rows // fine
    count = signal.shape[1] // groups
    half = count // 2
    wide = length + 2 * rows
    late = [rows - fine * (g + 1) for g in range(groups)]
    for g in range(groups - 1):
        signal[0 : late[g], g * count : (g + 1) * count] = jnp.zeros((late[g], count), signal.dtype)
    base[:, length:] = jnp.zeros((base.shape[0], 2 * rows), jnp.float32)
    for shift in range(chips):
        for which, block in enumerate((own[shift], pair[shift])):
            place = 2 * (chip ^ shift) + (core if which == 0 else 1 - core)
            value = block[0:rows, :]
            turned = jnp.concatenate([value[:, half:], value[:, :half]], axis=1)
            value = jnp.where(core == 0, value, turned)
            for g in range(groups):
                at = pl.multiple_of(place * rows + late[g], fine)
                signal[pl.ds(at, rows), g * count : (g + 1) * count] = value
            if packed:
                at = pl.multiple_of((devices - 1 - place) * rows, rows)
                base[:, pl.ds(at, rows)] = block[rows:, 0:rows].astype(jnp.float32)
    if not packed:
        base[:, 0:length] = taps_ref[...]

    def one_filter(k, carry):
        line = jnp.broadcast_to(base[pl.ds(k, 1), :], (8, wide))
        line = pltpu.roll(line, wide - fine + 1, 1, stride=1, stride_axis=0)
        for step in range(fine // 16):
            pieces = [pltpu.roll(line, 16 * step + 8 * h, 1)[:, : length + rows] for h in (0, 1)]
            at = pl.multiple_of(k * fine + 16 * step, 16)
            strip[pl.ds(at, 16), :] = jnp.concatenate(pieces, axis=0).astype(jnp.bfloat16)
        return carry

    lax.fori_loop(0, num, one_filter, 0, unroll=num if packed else 1)


def branch_kernel(chips, rows, fine, kind, *refs):
    signal, strip, mix_ref, pair_mix_ref, out_ref, feats = refs
    index = lax.axis_index("seq")
    other, part = aim(index // 2, index % 2, kind)
    devices = 2 * chips
    num, half, width = mix_ref.shape
    offset = (devices - 1 - (2 * other + part)) * rows

    def convolve(steps):
        depth = 2 * rows * steps
        left = strip[:, pl.ds(pl.multiple_of(offset, rows), depth)]
        total = jnp.dot(left, signal[0:depth, :], preferred_element_type=jnp.float32)
        for k in range(num):
            for which in range(2):
                for g in range(rows // fine):
                    to = (which * num + k) * half
                    at = (2 * g + which) * half
                    feats[g * fine : (g + 1) * fine, to : to + half] = total[
                        k * fine : (k + 1) * fine, at : at + half
                    ].astype(jnp.bfloat16)

    for steps in range(1, chips + 1):
        pl.when(other == steps - 1)(functools.partial(convolve, steps))
    total = project(feats, mix_ref, pair_mix_ref)
    out_ref[...] = total.astype(out_ref.dtype)


def shifted_kernel(chips, rows, shift_ref, *refs):
    signal, strip, mix_ref, pair_mix_ref, out_ref, sums = refs
    index = lax.axis_index("seq")
    other = (index // 2) ^ shift_ref[0]
    devices = 2 * chips
    num, half, width = mix_ref.shape
    offset = (devices - 1 - (2 * other + index % 2)) * rows
    sums[...] = jnp.zeros(sums.shape, jnp.float32)

    def add_tokens(step, carry):
        at = pl.multiple_of(2 * rows * step, 2 * rows)
        left = strip[:, pl.ds(pl.multiple_of(offset + at, rows), 2 * rows)]
        sums[...] += jnp.dot(
            left, signal[pl.ds(at, 2 * rows), :], preferred_element_type=jnp.float32
        )
        return carry

    lax.fori_loop(0, other + 1, add_tokens, 0)
    total = jnp.zeros((rows, width), jnp.float32)
    for k in range(num):
        found = sums[k * rows : (k + 1) * rows, :].astype(jnp.bfloat16)
        weight = jnp.concatenate([mix_ref[k], pair_mix_ref[k]], axis=0)
        total += jnp.dot(found, weight, preferred_element_type=jnp.float32)
    out_ref[...] = total.astype(out_ref.dtype)


def local(tokens, norm_gain, filters, mixing):
    rows, width = tokens.shape
    devices = lax.axis_size("seq")
    chips = devices // 2
    num, span = filters.shape
    length = devices * rows
    count = width // chips
    packed = count >= span
    relay = chips == 4 and packed and count % 256 == 0
    pair_mixing = swap(mixing, 1, devices)
    fine = 32 if relay else rows
    tall = rows + (EXTRA if packed else 0)
    blocks = kernel_call(
        norm_kernel,
        "norm",
        [jax.ShapeDtypeStruct((tall, count), jnp.bfloat16)] * chips,
        [HBM] * 3,
        8 * MIB,
        [
            pltpu.VMEM((rows, width), tokens.dtype),
            pltpu.VMEM((1, width), norm_gain.dtype),
            pltpu.VMEM((num, span), filters.dtype),
            pltpu.SemaphoreType.DMA((3,)),
        ],
    )(in_hbm(tokens), in_hbm(norm_gain.reshape(1, width)), in_hbm(filters))
    far = [swap(blocks[s], 2 * s, devices) for s in reversed(range(1, chips))]
    own = [blocks[0], *reversed(far)]
    near_mixing, first = kernel_call(
        stage_kernel,
        "stage",
        [
            jax.ShapeDtypeStruct(mixing.shape, mixing.dtype),
            jax.ShapeDtypeStruct(blocks[0].shape, blocks[0].dtype),
        ],
        [HBM, VMEM],
        8 * MIB,
        [pltpu.SemaphoreType.DMA(())],
    )(in_hbm(mixing), blocks[0])
    pair = [swap(block, 1, devices) for block in (first, *own[1:])]
    operands = [*own, *pair]
    specs = [VMEM] * (2 * chips)
    feats = pltpu.VMEM((rows, num * count), jnp.bfloat16)
    shapes = [
        jax.ShapeDtypeStruct((length + rows, rows // fine * count), jnp.bfloat16),
        jax.ShapeDtypeStruct((num * fine, length + rows), jnp.bfloat16),
    ]
    scratch = [pltpu.VMEM((EXTRA, length + 2 * rows), jnp.float32)]
    if not packed:
        taps = lax.all_gather(filters, "seq", axis=1, tiled=True)[:, ::-1]
        operands.append(jnp.pad(taps, ((0, EXTRA - num), (0, 0))))
        specs.append(VMEM)
    signal, strip = kernel_call(
        functools.partial(strip_kernel, chips, rows, num, fine, packed),
        "strip",
        shapes,
        specs,
        24 * MIB if relay else 48 * MIB,
        scratch,
    )(*operands)
    fixed = [signal, strip, near_mixing, pair_mixing]
    total = tokens.astype(jnp.float32)
    if relay:

        def branch(kind, dtype):
            return kernel_call(
                functools.partial(branch_kernel, chips, rows, fine, kind),
                "branch",
                jax.ShapeDtypeStruct((rows, width), dtype),
                [VMEM] * 4,
                24 * MIB,
                [feats],
            )(*fixed)

        pairs = [(c, q) for c in range(chips) for q in range(2)]
        across = [(2 * c + q, 2 * (c ^ (1 + q)) + 1 - q) for c, q in pairs]
        along = [(2 * c + q, 2 * (c ^ (1 + q)) + q) for c, q in pairs]
        far = lax.ppermute(branch("far", jnp.bfloat16), "seq", across)
        other = lax.ppermute(branch("other", jnp.bfloat16), "seq", across)
        same = (branch("same", jnp.float32) + far.astype(jnp.float32)).astype(jnp.bfloat16)
        same = lax.ppermute(same, "seq", along)
        total = total + branch("own", jnp.float32)
        sent = [other, same]
    else:

        def branch(shift):
            return kernel_call(
                functools.partial(shifted_kernel, chips, rows),
                "branch",
                jax.ShapeDtypeStruct((rows, width), jnp.bfloat16),
                [SMEM] + [VMEM] * 4,
                48 * MIB,
                [pltpu.VMEM((num * rows, count), jnp.float32)],
            )(shift.reshape(1), *fixed)

        parts = lax.map(branch, jnp.arange(chips, dtype=jnp.int32))
        sent = [parts[0]] + [swap(parts[s], 2 * s, devices) for s in range(1, chips)]
    for value in sent:
        total = total + value.astype(jnp.float32)
    return total.astype(jnp.bfloat16)


def solution(mesh):
    in_specs = (P(("dp", "seq"), None), P(), P(None, "seq"), P(None, "seq", None))
    out_specs = P(("dp", "seq"), None)
    return jax.shard_map(local, mesh=mesh, in_specs=in_specs, out_specs=out_specs, check_vma=False)
```

```python
import functools

import jax
import jax.numpy as jnp
from jax import lax
from jax.experimental import pallas as pl
from jax.experimental.pallas import tpu as pltpu
from jax.sharding import PartitionSpec as P

MIB = 1024 * 1024
EXTRA = 16
VMEM = pl.BlockSpec(memory_space=pltpu.VMEM)
SMEM = pl.BlockSpec(memory_space=pltpu.SMEM)
HBM = pl.BlockSpec(memory_space=pltpu.HBM)


def swap(value, bits, size):
    return lax.ppermute(value, "seq", [(i, i ^ bits) for i in range(size)])


def kernel_call(kernel, name, out_shape, specs, limit, scratch=()):
    return pl.pallas_call(
        kernel,
        out_shape=out_shape,
        in_specs=specs,
        out_specs=jax.tree.map(lambda _: VMEM, out_shape),
        scratch_shapes=scratch,
        compiler_params=pltpu.CompilerParams(vmem_limit_bytes=limit),
        name=name,
    )


def in_hbm(value):
    return pltpu.with_memory_space_constraint(value, pltpu.HBM)


def norm_kernel(tokens_hbm, gain_hbm, filters_hbm, *refs):
    *out_refs, tokens_ref, gain_ref, filters_ref, sems = refs
    pairs = ((filters_hbm, filters_ref), (gain_hbm, gain_ref), (tokens_hbm, tokens_ref))
    copies = [pltpu.make_async_copy(a, b, sems.at[i]) for i, (a, b) in enumerate(pairs)]
    for copy in copies:
        copy.start()
    chip = lax.axis_index("seq") // 2
    rows, width = tokens_ref.shape
    chips = len(out_refs)
    count = width // chips
    num, span = filters_ref.shape
    packed = out_refs[0].shape[0] > rows
    copies[0].wait()
    if packed:
        flip = (
            lax.broadcasted_iota(jnp.int32, (span, span), 0)
            + lax.broadcasted_iota(jnp.int32, (span, span), 1)
            == span - 1
        ).astype(jnp.bfloat16)
        taps = jnp.dot(
            filters_ref[...].astype(jnp.bfloat16), flip, preferred_element_type=jnp.float32
        )
        taps = jnp.concatenate([taps, jnp.zeros((EXTRA - num, span), jnp.float32)], axis=0)
        taps = jnp.concatenate([taps, jnp.zeros((EXTRA, count - span), jnp.float32)], axis=1)
        taps = taps.astype(jnp.bfloat16)
    copies[1].wait()
    copies[2].wait()
    values = tokens_ref[...].astype(jnp.float32)
    scale = lax.rsqrt(jnp.mean(values * values, axis=1, keepdims=True) + 1e-05)
    normed = (values * scale * gain_ref[...]).astype(jnp.bfloat16)
    for part in range(chips):
        for shift, out_ref in enumerate(out_refs):

            @pl.when(chip == part ^ shift)
            def _(part=part, out_ref=out_ref):
                out_ref[0:rows, :] = normed[:, part * count : (part + 1) * count]

    if packed:
        for out_ref in out_refs:
            out_ref[rows:, :] = taps


def stage_kernel(mix_hbm, block_ref, mix_ref, out_ref, sem):
    copy = pltpu.make_async_copy(mix_hbm, mix_ref, sem)
    copy.start()
    out_ref[...] = block_ref[...]
    copy.wait()


def aim(chip, core, kind):
    if kind == "far":
        return chip ^ 3, core
    if kind == "own":
        return chip, core
    return chip ^ (1 + core), core if kind == "early" else 1 - core


def project(feats, mix_ref, pair_mix_ref):
    num, half, width = mix_ref.shape
    both = num * half
    return jnp.dot(
        feats[:, :both],
        mix_ref[...].reshape(both, width),
        preferred_element_type=jnp.float32,
    ) + jnp.dot(
        feats[:, both:],
        pair_mix_ref[...].reshape(both, width),
        preferred_element_type=jnp.float32,
    )


def block_places(chips, shifts):
    index = lax.axis_index("seq")
    chip = index // 2
    core = index % 2
    first = [core if s == 0 else 1 - core for s in shifts]
    return [(2 * (chip ^ s) + q, 2 * (chip ^ s) + 1 - q) for s, q in zip(shifts, first, strict=True)]


def rotate_taps(block_refs, places, rows, num, fine, out_ref, devices):
    for block, place in zip(block_refs, places, strict=True):
        taps = block[rows:, 0:rows].astype(jnp.float32)
        at = pl.multiple_of((devices - 1 - place) * rows, rows)
        for k in range(num):
            line = jnp.broadcast_to(taps[k : k + 1, :], (8, rows))
            line = pltpu.roll(line, rows - fine + 1, 1, stride=1, stride_axis=0)
            lines = [line] + [pltpu.roll(line, step, 1) for step in range(8, fine, 8)]
            out_ref[k * fine : (k + 1) * fine, pl.ds(at, rows)] = jnp.concatenate(
                lines, axis=0
            ).astype(jnp.bfloat16)


def rotate_kernel(chips, shifts, rows, num, fine, *refs):
    *blocks, out_ref = refs
    places = [place for pair in zip(*block_places(chips, shifts), strict=True) for place in pair]
    rotate_taps(blocks, places, rows, num, fine, out_ref, 2 * chips)


def merge_kernel(chips, shifts, done, rows, num, fine, *refs):
    own = refs[:chips]
    pair = refs[chips : 2 * chips]
    turned_ref, signal, strip, lines = refs[2 * chips :]
    devices = 2 * chips
    length = devices * rows
    groups = rows // fine
    count = signal.shape[1] // groups
    half = count // 2
    core = lax.axis_index("seq") % 2
    late = [rows - fine * (g + 1) for g in range(groups)]
    for g in range(groups - 1):
        signal[0 : late[g], g * count : (g + 1) * count] = jnp.zeros((late[g], count), signal.dtype)
    places = block_places(chips, shifts)
    for own_block, pair_block, both in zip(own, pair, places, strict=True):
        for block, place in zip((own_block, pair_block), both, strict=True):
            value = block[0:rows, :]
            turned = jnp.concatenate([value[:, half:], value[:, :half]], axis=1)
            value = jnp.where(core == 0, value, turned)
            for g in range(groups):
                at = pl.multiple_of(place * rows + late[g], fine)
                signal[pl.ds(at, rows), g * count : (g + 1) * count] = value
    lines[...] = turned_ref[...]
    for shift in range(done, chips):
        rotate_taps((own[shift], pair[shift]), places[shift], rows, num, fine, lines, devices)
    row = lax.broadcasted_iota(jnp.int32, (fine, rows), 0)
    lane = lax.broadcasted_iota(jnp.int32, (fine, rows), 1)
    here = lane - row < rows - fine + 1
    nothing = jnp.zeros((fine, rows), jnp.bfloat16)
    for k in range(num):
        cut = slice(k * fine, (k + 1) * fine)
        parts = [lines[cut, b * rows : (b + 1) * rows] for b in range(devices)] + [nothing]
        for b in range(devices):
            strip[cut, b * rows : (b + 1) * rows] = jnp.where(here, parts[b], parts[b + 1])
        strip[cut, length:] = nothing


def strip_kernel(chips, rows, num, *refs):
    own = refs[:chips]
    pair = refs[chips : 2 * chips]
    taps_ref, signal, strip = refs[2 * chips :]
    length = 2 * chips * rows
    half = signal.shape[1] // 2
    wide = length + 2 * rows
    core = lax.axis_index("seq") % 2
    places = block_places(chips, range(chips))
    for own_block, pair_block, both in zip(own, pair, places, strict=True):
        for block, place in zip((own_block, pair_block), both, strict=True):
            value = block[...]
            turned = jnp.concatenate([value[:, half:], value[:, :half]], axis=1)
            value = jnp.where(core == 0, value, turned)
            signal[pl.ds(pl.multiple_of(place * rows, rows), rows), :] = value

    def one_filter(k, carry):
        line = jnp.broadcast_to(taps_ref[pl.ds(k, 1), :], (8, wide))
        line = pltpu.roll(line, wide - rows + 1, 1, stride=1, stride_axis=0)
        for step in range(rows // 16):
            pieces = [pltpu.roll(line, 16 * step + 8 * h, 1)[:, : length + rows] for h in (0, 1)]
            at = pl.multiple_of(k * rows + 16 * step, 16)
            strip[pl.ds(at, 16), :] = jnp.concatenate(pieces, axis=0).astype(jnp.bfloat16)
        return carry

    lax.fori_loop(0, num, one_filter, 0)


def branch_kernel(chips, rows, fine, kind, *refs):
    signal, strip, mix_ref, pair_mix_ref, out_ref, feats = refs
    index = lax.axis_index("seq")
    other, part = aim(index // 2, index % 2, kind)
    devices = 2 * chips
    num, half, width = mix_ref.shape
    offset = (devices - 1 - (2 * other + part)) * rows

    def convolve(steps):
        depth = 2 * rows * steps
        left = strip[:, pl.ds(pl.multiple_of(offset, rows), depth)]
        total = jnp.dot(left, signal[0:depth, :], preferred_element_type=jnp.float32)
        for k in range(num):
            for which in range(2):
                for g in range(rows // fine):
                    to = (which * num + k) * half
                    at = (2 * g + which) * half
                    feats[g * fine : (g + 1) * fine, to : to + half] = total[
                        k * fine : (k + 1) * fine, at : at + half
                    ].astype(jnp.bfloat16)

    for steps in range(1, chips + 1):
        pl.when(other == steps - 1)(functools.partial(convolve, steps))
    total = project(feats, mix_ref, pair_mix_ref)
    out_ref[...] = total.astype(out_ref.dtype)


def shifted_kernel(chips, rows, shift_ref, *refs):
    signal, strip, mix_ref, pair_mix_ref, out_ref, sums = refs
    index = lax.axis_index("seq")
    other = (index // 2) ^ shift_ref[0]
    devices = 2 * chips
    num, half, width = mix_ref.shape
    offset = (devices - 1 - (2 * other + index % 2)) * rows
    sums[...] = jnp.zeros(sums.shape, jnp.float32)

    def add_tokens(step, carry):
        at = pl.multiple_of(2 * rows * step, 2 * rows)
        left = strip[:, pl.ds(pl.multiple_of(offset + at, rows), 2 * rows)]
        sums[...] += jnp.dot(
            left, signal[pl.ds(at, 2 * rows), :], preferred_element_type=jnp.float32
        )
        return carry

    lax.fori_loop(0, other + 1, add_tokens, 0)
    total = jnp.zeros((rows, width), jnp.float32)
    for k in range(num):
        found = sums[k * rows : (k + 1) * rows, :].astype(jnp.bfloat16)
        weight = jnp.concatenate([mix_ref[k], pair_mix_ref[k]], axis=0)
        total += jnp.dot(found, weight, preferred_element_type=jnp.float32)
    out_ref[...] = total.astype(out_ref.dtype)


def local(tokens, norm_gain, filters, mixing):
    rows, width = tokens.shape
    devices = lax.axis_size("seq")
    chips = devices // 2
    num, span = filters.shape
    length = devices * rows
    count = width // chips
    relay = chips == 4 and count % 256 == 0 and span == rows and num <= EXTRA
    pair_mixing = swap(mixing, 1, devices)
    fine = 32 if relay else rows
    tall = rows + (EXTRA if relay else 0)
    blocks = kernel_call(
        norm_kernel,
        "norm",
        [jax.ShapeDtypeStruct((tall, count), jnp.bfloat16)] * chips,
        [HBM] * 3,
        8 * MIB,
        [
            pltpu.VMEM((rows, width), tokens.dtype),
            pltpu.VMEM((1, width), norm_gain.dtype),
            pltpu.VMEM((num, span), filters.dtype),
            pltpu.SemaphoreType.DMA((3,)),
        ],
    )(in_hbm(tokens), in_hbm(norm_gain.reshape(1, width)), in_hbm(filters))
    near_mixing, first = kernel_call(
        stage_kernel,
        "stage",
        [
            jax.ShapeDtypeStruct(mixing.shape, mixing.dtype),
            jax.ShapeDtypeStruct(blocks[0].shape, blocks[0].dtype),
        ],
        [HBM, VMEM],
        8 * MIB,
        [pltpu.SemaphoreType.DMA(())],
    )(in_hbm(mixing), blocks[0])
    work = 2 * num * rows * count * (width + length)
    shifts = [0, 3, 1, 2] if relay else list(range(chips))
    own = {s: swap(blocks[s], 2 * s + 1, devices) for s in reversed(shifts) if s}
    own[0] = first
    pair = {s: swap(own[s], 1, devices) for s in shifts}
    own[0] = blocks[0]
    ends = [own[s] for s in shifts] + [pair[s] for s in shifts]
    shapes = [
        jax.ShapeDtypeStruct((length + rows, rows // fine * count), jnp.bfloat16),
        jax.ShapeDtypeStruct((num * fine, length + rows), jnp.bfloat16),
    ]
    if relay:
        done = chips - 1
        lines = jax.ShapeDtypeStruct((num * fine, length), jnp.bfloat16)
        ready = ends[:done] + ends[chips : chips + done]
        turned = kernel_call(
            functools.partial(rotate_kernel, chips, shifts[:done], rows, num, fine),
            "rotate",
            lines,
            [VMEM] * len(ready),
            8 * MIB,
        )(*ready)
        signal, strip = kernel_call(
            functools.partial(merge_kernel, chips, shifts, done, rows, num, fine),
            "merge",
            shapes,
            [VMEM] * (2 * chips + 1),
            16 * MIB,
            [pltpu.VMEM(lines.shape, lines.dtype)],
        )(*ends, turned)
    else:
        taps = lax.all_gather(filters, "seq", axis=1, tiled=True)[:, ::-1]
        taps = jnp.pad(taps, ((0, EXTRA - num), (0, 2 * rows)))
        signal, strip = kernel_call(
            functools.partial(strip_kernel, chips, rows, num),
            "strip",
            shapes,
            [VMEM] * (2 * chips + 1),
            48 * MIB,
        )(*ends, taps)
    fixed = [signal, strip, near_mixing, pair_mixing]
    total = tokens.astype(jnp.float32)
    if relay:

        def branch(kind, dtype):
            return kernel_call(
                functools.partial(branch_kernel, chips, rows, fine, kind),
                "branch",
                jax.ShapeDtypeStruct((rows, width), dtype),
                [VMEM] * 4,
                24 * MIB,
                [pltpu.VMEM((rows, num * count), jnp.bfloat16)],
            )(*fixed)

        pairs = [(c, q) for c in range(chips) for q in range(2)]
        across = [(2 * c + q, 2 * (c ^ (1 + q)) + 1 - q) for c, q in pairs]
        along = [(2 * c + q, 2 * (c ^ (1 + q)) + q) for c, q in pairs]
        far = lax.ppermute(branch("far", jnp.bfloat16), "seq", across)
        early = lax.ppermute(branch("early", jnp.bfloat16), "seq", along)
        late = (branch("late", jnp.float32) + far.astype(jnp.float32)).astype(jnp.bfloat16)
        late = lax.ppermute(late, "seq", across)
        total = total + branch("own", jnp.float32)
        sent = [early, late]
    else:

        def branch(shift):
            return kernel_call(
                functools.partial(shifted_kernel, chips, rows),
                "branch",
                jax.ShapeDtypeStruct((rows, width), jnp.bfloat16),
                [SMEM] + [VMEM] * 4,
                48 * MIB,
                [pltpu.VMEM((num * rows, count), jnp.float32)],
            )(shift.reshape(1), *fixed)

        parts = lax.map(branch, jnp.arange(chips, dtype=jnp.int32))
        sent = [parts[0]] + [swap(parts[s], 2 * s, devices) for s in range(1, chips)]
    for value in sent:
        total = total + value.astype(jnp.float32)
    return total.astype(jnp.bfloat16)


def solution(mesh):
    in_specs = (P(("dp", "seq"), None), P(), P(None, "seq"), P(None, "seq", None))
    out_specs = P(("dp", "seq"), None)
    return jax.shard_map(local, mesh=mesh, in_specs=in_specs, out_specs=out_specs, check_vma=False)
```

```python
import functools

import jax
import jax.numpy as jnp
from jax import lax
from jax.experimental import pallas as pl
from jax.experimental.pallas import tpu as pltpu
from jax.sharding import PartitionSpec as P

MIB = 1024 * 1024
EXTRA = 16
VMEM = pl.BlockSpec(memory_space=pltpu.VMEM)
SMEM = pl.BlockSpec(memory_space=pltpu.SMEM)
HBM = pl.BlockSpec(memory_space=pltpu.HBM)


def swap(value, bits, size):
    return lax.ppermute(value, "seq", [(i, i ^ bits) for i in range(size)])


def kernel_call(kernel, name, out_shape, specs, limit, scratch=()):
    return pl.pallas_call(
        kernel,
        out_shape=out_shape,
        in_specs=specs,
        out_specs=jax.tree.map(lambda _: VMEM, out_shape),
        scratch_shapes=scratch,
        compiler_params=pltpu.CompilerParams(vmem_limit_bytes=limit),
        name=name,
    )


def in_hbm(value):
    return pltpu.with_memory_space_constraint(value, pltpu.HBM)


def norm_kernel(tokens_hbm, gain_hbm, filters_hbm, *refs):
    *out_refs, tokens_ref, gain_ref, filters_ref, sems = refs
    pairs = ((filters_hbm, filters_ref), (gain_hbm, gain_ref), (tokens_hbm, tokens_ref))
    copies = [pltpu.make_async_copy(a, b, sems.at[i]) for i, (a, b) in enumerate(pairs)]
    for copy in copies:
        copy.start()
    chip = lax.axis_index("seq") // 2
    rows, width = tokens_ref.shape
    chips = len(out_refs)
    count = width // chips
    num, span = filters_ref.shape
    packed = out_refs[0].shape[0] > rows
    copies[0].wait()
    if packed:
        flip = (
            lax.broadcasted_iota(jnp.int32, (span, span), 0)
            + lax.broadcasted_iota(jnp.int32, (span, span), 1)
            == span - 1
        ).astype(jnp.bfloat16)
        taps = jnp.dot(
            filters_ref[...].astype(jnp.bfloat16), flip, preferred_element_type=jnp.float32
        )
        taps = jnp.concatenate([taps, jnp.zeros((EXTRA - num, span), jnp.float32)], axis=0)
        taps = jnp.concatenate([taps, jnp.zeros((EXTRA, count - span), jnp.float32)], axis=1)
        taps = taps.astype(jnp.bfloat16)
    copies[1].wait()
    copies[2].wait()
    values = tokens_ref[...].astype(jnp.float32)
    scale = lax.rsqrt(jnp.mean(values * values, axis=1, keepdims=True) + 1e-05)
    normed = (values * scale * gain_ref[...]).astype(jnp.bfloat16)
    for part in range(chips):
        for shift, out_ref in enumerate(out_refs):

            @pl.when(chip == part ^ shift)
            def _(part=part, out_ref=out_ref):
                out_ref[0:rows, :] = normed[:, part * count : (part + 1) * count]

    if packed:
        for out_ref in out_refs:
            out_ref[rows:, :] = taps


def stage_kernel(mix_hbm, block_ref, mix_ref, out_ref, sem):
    copy = pltpu.make_async_copy(mix_hbm, mix_ref, sem)
    copy.start()
    out_ref[...] = block_ref[...]
    copy.wait()


def aim(chip, core, kind):
    if kind == "far":
        return chip ^ 3, core
    if kind == "own":
        return chip, core
    return chip ^ (1 + core), core if kind == "early" else 1 - core


def project(feats, mix_ref, pair_mix_ref):
    num, half, width = mix_ref.shape
    both = num * half
    return jnp.dot(
        feats[:, :both],
        mix_ref[...].reshape(both, width),
        preferred_element_type=jnp.float32,
    ) + jnp.dot(
        feats[:, both:],
        pair_mix_ref[...].reshape(both, width),
        preferred_element_type=jnp.float32,
    )


def block_places(chips, shifts):
    index = lax.axis_index("seq")
    chip = index // 2
    core = index % 2
    first = [core if s == 0 else 1 - core for s in shifts]
    return [(2 * (chip ^ s) + q, 2 * (chip ^ s) + 1 - q) for s, q in zip(shifts, first, strict=True)]


def ordered(value, core):
    half = value.shape[1] // 2
    turned = jnp.concatenate([value[:, half:], value[:, :half]], axis=1)
    return jnp.where(core == 0, value, turned)


def merge_kernel(chips, shifts, rows, num, fine, *refs):
    own = refs[:chips]
    pair = refs[chips : 2 * chips]
    signal, strip, base = refs[2 * chips :]
    devices = 2 * chips
    length = devices * rows
    groups = rows // fine
    count = signal.shape[1] // groups
    wide = length + 2 * rows
    core = lax.axis_index("seq") % 2
    late = [rows - fine * (g + 1) for g in range(groups)]
    for g in range(groups - 1):
        signal[0 : late[g], g * count : (g + 1) * count] = jnp.zeros((late[g], count), signal.dtype)
    base[:, length:] = jnp.zeros((EXTRA, 2 * rows), jnp.float32)
    places = block_places(chips, shifts)
    for own_block, pair_block, both in zip(own, pair, places, strict=True):
        for block, place in zip((own_block, pair_block), both, strict=True):
            value = ordered(block[0:rows, :], core)
            for g in range(groups):
                at = pl.multiple_of(place * rows + late[g], fine)
                signal[pl.ds(at, rows), g * count : (g + 1) * count] = value
            at = pl.multiple_of((devices - 1 - place) * rows, rows)
            base[:, pl.ds(at, rows)] = block[rows:, 0:rows].astype(jnp.float32)
    for k in range(num):
        line = jnp.broadcast_to(base[k : k + 1, :], (8, wide))
        line = pltpu.roll(line, wide - fine + 1, 1, stride=1, stride_axis=0)
        for step in range(0, fine, 16):
            pieces = [pltpu.roll(line, step + h, 1)[:, : length + rows] for h in (0, 8)]
            at = k * fine + step
            strip[at : at + 16, :] = jnp.concatenate(pieces, axis=0).astype(jnp.bfloat16)


def strip_kernel(chips, rows, num, *refs):
    own = refs[:chips]
    pair = refs[chips : 2 * chips]
    taps_ref, signal, strip = refs[2 * chips :]
    length = 2 * chips * rows
    half = signal.shape[1] // 2
    wide = length + 2 * rows
    core = lax.axis_index("seq") % 2
    places = block_places(chips, range(chips))
    for own_block, pair_block, both in zip(own, pair, places, strict=True):
        for block, place in zip((own_block, pair_block), both, strict=True):
            value = block[...]
            turned = jnp.concatenate([value[:, half:], value[:, :half]], axis=1)
            value = jnp.where(core == 0, value, turned)
            signal[pl.ds(pl.multiple_of(place * rows, rows), rows), :] = value

    def one_filter(k, carry):
        line = jnp.broadcast_to(taps_ref[pl.ds(k, 1), :], (8, wide))
        line = pltpu.roll(line, wide - rows + 1, 1, stride=1, stride_axis=0)
        for step in range(rows // 16):
            pieces = [pltpu.roll(line, 16 * step + 8 * h, 1)[:, : length + rows] for h in (0, 1)]
            at = pl.multiple_of(k * rows + 16 * step, 16)
            strip[pl.ds(at, 16), :] = jnp.concatenate(pieces, axis=0).astype(jnp.bfloat16)
        return carry

    lax.fori_loop(0, num, one_filter, 0)


def branch_kernel(chips, rows, fine, kind, *refs):
    signal, strip, mix_ref, pair_mix_ref, out_ref, feats = refs
    index = lax.axis_index("seq")
    other, part = aim(index // 2, index % 2, kind)
    devices = 2 * chips
    num, half, width = mix_ref.shape
    offset = (devices - 1 - (2 * other + part)) * rows

    def convolve(steps):
        depth = 2 * rows * steps
        left = strip[:, pl.ds(pl.multiple_of(offset, rows), depth)]
        total = jnp.dot(left, signal[0:depth, :], preferred_element_type=jnp.float32)
        for k in range(num):
            for which in range(2):
                for g in range(rows // fine):
                    to = (which * num + k) * half
                    at = (2 * g + which) * half
                    feats[g * fine : (g + 1) * fine, to : to + half] = total[
                        k * fine : (k + 1) * fine, at : at + half
                    ].astype(jnp.bfloat16)

    for steps in range(1, chips + 1):
        pl.when(other == steps - 1)(functools.partial(convolve, steps))
    total = project(feats, mix_ref, pair_mix_ref)
    out_ref[...] = total.astype(out_ref.dtype)


def shifted_kernel(chips, rows, shift_ref, *refs):
    signal, strip, mix_ref, pair_mix_ref, out_ref, sums = refs
    index = lax.axis_index("seq")
    other = (index // 2) ^ shift_ref[0]
    devices = 2 * chips
    num, half, width = mix_ref.shape
    offset = (devices - 1 - (2 * other + index % 2)) * rows
    sums[...] = jnp.zeros(sums.shape, jnp.float32)

    def add_tokens(step, carry):
        at = pl.multiple_of(2 * rows * step, 2 * rows)
        left = strip[:, pl.ds(pl.multiple_of(offset + at, rows), 2 * rows)]
        sums[...] += jnp.dot(
            left, signal[pl.ds(at, 2 * rows), :], preferred_element_type=jnp.float32
        )
        return carry

    lax.fori_loop(0, other + 1, add_tokens, 0)
    total = jnp.zeros((rows, width), jnp.float32)
    for k in range(num):
        found = sums[k * rows : (k + 1) * rows, :].astype(jnp.bfloat16)
        weight = jnp.concatenate([mix_ref[k], pair_mix_ref[k]], axis=0)
        total += jnp.dot(found, weight, preferred_element_type=jnp.float32)
    out_ref[...] = total.astype(out_ref.dtype)


def local(tokens, norm_gain, filters, mixing):
    rows, width = tokens.shape
    devices = lax.axis_size("seq")
    chips = devices // 2
    num, span = filters.shape
    length = devices * rows
    count = width // chips
    relay = chips == 4 and count % 256 == 0 and span == rows and num <= EXTRA
    pair_mixing = swap(mixing, 1, devices)
    fine = 32 if relay else rows
    tall = rows + (EXTRA if relay else 0)
    blocks = kernel_call(
        norm_kernel,
        "norm",
        [jax.ShapeDtypeStruct((tall, count), jnp.bfloat16)] * chips,
        [HBM] * 3,
        8 * MIB,
        [
            pltpu.VMEM((rows, width), tokens.dtype),
            pltpu.VMEM((1, width), norm_gain.dtype),
            pltpu.VMEM((num, span), filters.dtype),
            pltpu.SemaphoreType.DMA((3,)),
        ],
    )(in_hbm(tokens), in_hbm(norm_gain.reshape(1, width)), in_hbm(filters))
    near_mixing, first = kernel_call(
        stage_kernel,
        "stage",
        [
            jax.ShapeDtypeStruct(mixing.shape, mixing.dtype),
            jax.ShapeDtypeStruct(blocks[0].shape, blocks[0].dtype),
        ],
        [HBM, VMEM],
        8 * MIB,
        [pltpu.SemaphoreType.DMA(())],
    )(in_hbm(mixing), blocks[0])
    work = 2 * num * rows * count * (width + length)
    shifts = [0, 3, 1, 2] if relay else list(range(chips))
    own = {s: swap(blocks[s], 2 * s + 1, devices) for s in reversed(shifts) if s}
    own[0] = first
    pair = {s: swap(own[s], 1, devices) for s in shifts}
    own[0] = blocks[0]
    ends = [own[s] for s in shifts] + [pair[s] for s in shifts]
    shapes = [
        jax.ShapeDtypeStruct((length + rows, rows // fine * count), jnp.bfloat16),
        jax.ShapeDtypeStruct((num * fine, length + rows), jnp.bfloat16),
    ]
    if relay:
        signal, strip = kernel_call(
            functools.partial(merge_kernel, chips, shifts, rows, num, fine),
            "merge",
            shapes,
            [VMEM] * (2 * chips),
            16 * MIB,
            [pltpu.VMEM((EXTRA, length + 2 * rows), jnp.float32)],
        )(*ends)
    else:
        taps = lax.all_gather(filters, "seq", axis=1, tiled=True)[:, ::-1]
        taps = jnp.pad(taps, ((0, EXTRA - num), (0, 2 * rows)))
        signal, strip = kernel_call(
            functools.partial(strip_kernel, chips, rows, num),
            "strip",
            shapes,
            [VMEM] * (2 * chips + 1),
            48 * MIB,
        )(*ends, taps)
    fixed = [signal, strip, near_mixing, pair_mixing]
    total = tokens.astype(jnp.float32)
    if relay:

        def branch(kind, dtype):
            return kernel_call(
                functools.partial(branch_kernel, chips, rows, fine, kind),
                "branch",
                jax.ShapeDtypeStruct((rows, width), dtype),
                [VMEM] * 4,
                24 * MIB,
                [pltpu.VMEM((rows, num * count), jnp.bfloat16)],
            )(*fixed)

        pairs = [(c, q) for c in range(chips) for q in range(2)]
        across = [(2 * c + q, 2 * (c ^ (1 + q)) + 1 - q) for c, q in pairs]
        along = [(2 * c + q, 2 * (c ^ (1 + q)) + q) for c, q in pairs]
        far = lax.ppermute(branch("far", jnp.bfloat16), "seq", across)
        early = lax.ppermute(branch("early", jnp.bfloat16), "seq", along)
        late = (branch("late", jnp.float32) + far.astype(jnp.float32)).astype(jnp.bfloat16)
        late = lax.ppermute(late, "seq", across)
        total = total + branch("own", jnp.float32)
        sent = [early, late]
    else:

        def branch(shift):
            return kernel_call(
                functools.partial(shifted_kernel, chips, rows),
                "branch",
                jax.ShapeDtypeStruct((rows, width), jnp.bfloat16),
                [SMEM] + [VMEM] * 4,
                48 * MIB,
                [pltpu.VMEM((num * rows, count), jnp.float32)],
            )(shift.reshape(1), *fixed)

        parts = lax.map(branch, jnp.arange(chips, dtype=jnp.int32))
        sent = [parts[0]] + [swap(parts[s], 2 * s, devices) for s in range(1, chips)]
    for value in sent:
        total = total + value.astype(jnp.float32)
    return total.astype(jnp.bfloat16)


def solution(mesh):
    in_specs = (P(("dp", "seq"), None), P(), P(None, "seq"), P(None, "seq", None))
    out_specs = P(("dp", "seq"), None)
    return jax.shard_map(local, mesh=mesh, in_specs=in_specs, out_specs=out_specs, check_vma=False)
```

```python
import functools

import jax
import jax.numpy as jnp
from jax import lax
from jax.experimental import pallas as pl
from jax.experimental.pallas import tpu as pltpu
from jax.sharding import PartitionSpec as P

MIB = 1024 * 1024
EXTRA = 16
VMEM = pl.BlockSpec(memory_space=pltpu.VMEM)
SMEM = pl.BlockSpec(memory_space=pltpu.SMEM)
HBM = pl.BlockSpec(memory_space=pltpu.HBM)


def swap(value, bits, size):
    return lax.ppermute(value, "seq", [(i, i ^ bits) for i in range(size)])


def kernel_call(kernel, name, out_shape, specs, limit, scratch=()):
    return pl.pallas_call(
        kernel,
        out_shape=out_shape,
        in_specs=specs,
        out_specs=jax.tree.map(lambda _: VMEM, out_shape),
        scratch_shapes=scratch,
        compiler_params=pltpu.CompilerParams(vmem_limit_bytes=limit),
        name=name,
    )


def in_hbm(value):
    return pltpu.with_memory_space_constraint(value, pltpu.HBM)


def norm_kernel(tokens_hbm, gain_hbm, filters_hbm, *refs):
    *out_refs, tokens_ref, gain_ref, filters_ref, sems = refs
    pairs = ((filters_hbm, filters_ref), (gain_hbm, gain_ref), (tokens_hbm, tokens_ref))
    copies = [pltpu.make_async_copy(a, b, sems.at[i]) for i, (a, b) in enumerate(pairs)]
    for copy in copies:
        copy.start()
    chip = lax.axis_index("seq") // 2
    rows, width = tokens_ref.shape
    chips = len(out_refs)
    count = width // chips
    num, span = filters_ref.shape
    packed = out_refs[0].shape[0] < rows
    copies[0].wait()
    if packed:
        flip = (
            lax.broadcasted_iota(jnp.int32, (span, span), 0)
            + lax.broadcasted_iota(jnp.int32, (span, span), 1)
            == span - 1
        ).astype(jnp.bfloat16)
        taps = jnp.dot(
            filters_ref[...].astype(jnp.bfloat16), flip, preferred_element_type=jnp.float32
        )
        taps = jnp.concatenate([taps, jnp.zeros((EXTRA - num, span), jnp.float32)], axis=0)
        for out_ref in out_refs:
            out_ref[:, rows // EXTRA * count :] = taps.astype(jnp.bfloat16)
    copies[1].wait()
    copies[2].wait()
    values = tokens_ref[...].astype(jnp.float32)
    scale = lax.rsqrt(jnp.mean(values * values, axis=1, keepdims=True) + 1e-05)
    normed = (values * scale * gain_ref[...]).astype(jnp.bfloat16)
    for part in range(chips):
        for shift, out_ref in enumerate(out_refs):

            @pl.when(chip == part ^ shift)
            def _(part=part, out_ref=out_ref):
                value = normed[:, part * count : (part + 1) * count]
                if not packed:
                    out_ref[...] = value
                    return
                for g in range(rows // EXTRA):
                    out_ref[:, g * count : (g + 1) * count] = value[g * EXTRA : (g + 1) * EXTRA]


def stage_kernel(mix_hbm, block_ref, mix_ref, out_ref, sem):
    copy = pltpu.make_async_copy(mix_hbm, mix_ref, sem)
    copy.start()
    out_ref[...] = block_ref[...]
    copy.wait()


def aim(chip, core, kind):
    if kind == "far":
        return chip ^ 3, core
    if kind == "own":
        return chip, core
    return chip ^ (1 + core), core if kind == "early" else 1 - core


def project(feats, mix_ref, pair_mix_ref):
    num, half, width = mix_ref.shape
    both = num * half
    return jnp.dot(
        feats[:, :both],
        mix_ref[...].reshape(both, width),
        preferred_element_type=jnp.float32,
    ) + jnp.dot(
        feats[:, both:],
        pair_mix_ref[...].reshape(both, width),
        preferred_element_type=jnp.float32,
    )


def block_places(chips, shifts):
    index = lax.axis_index("seq")
    chip = index // 2
    core = index % 2
    first = [core if s == 0 else 1 - core for s in shifts]
    return [(2 * (chip ^ s) + q, 2 * (chip ^ s) + 1 - q) for s, q in zip(shifts, first, strict=True)]


def ordered(value, core):
    half = value.shape[1] // 2
    turned = jnp.concatenate([value[:, half:], value[:, :half]], axis=1)
    return jnp.where(core == 0, value, turned)


def merge_kernel(chips, shifts, rows, num, fine, *refs):
    own = refs[:chips]
    pair = refs[chips : 2 * chips]
    signal, strip, base = refs[2 * chips :]
    devices = 2 * chips
    length = devices * rows
    groups = rows // fine
    count = signal.shape[1] // groups
    core = lax.axis_index("seq") % 2
    late = [rows - fine * (g + 1) for g in range(groups)]
    for g in range(groups - 1):
        signal[0 : late[g], g * count : (g + 1) * count] = jnp.zeros((late[g], count), signal.dtype)
    places = block_places(chips, shifts)
    for own_block, pair_block, both in zip(own, pair, places, strict=True):
        for block, place in zip((own_block, pair_block), both, strict=True):
            for part in range(rows // EXTRA):
                value = ordered(block[:, part * count : (part + 1) * count], core)
                for g in range(groups):
                    at = pl.multiple_of(place * rows + late[g] + part * EXTRA, EXTRA)
                    signal[pl.ds(at, EXTRA), g * count : (g + 1) * count] = value
            at = pl.multiple_of((devices - 1 - place) * rows, rows)
            base[:, pl.ds(at, rows)] = block[:, rows // EXTRA * count :].astype(jnp.float32)
    row = lax.broadcasted_iota(jnp.int32, (fine, rows), 0)
    lane = lax.broadcasted_iota(jnp.int32, (fine, rows), 1)
    kept = lane - row <= rows - fine
    strip[:, length:] = jnp.zeros((num * fine, rows), jnp.bfloat16)
    for k in range(num):
        line = jnp.broadcast_to(base[k : k + 1, :], (8, length))
        line = pltpu.roll(line, length - fine + 1, 1, stride=1, stride_axis=0)
        lines = [line] + [pltpu.roll(line, step, 1) for step in range(8, fine, 8)]
        whole = jnp.concatenate(lines, axis=0)
        cut = slice(k * fine, (k + 1) * fine)
        strip[cut, : length - rows] = whole[:, : length - rows].astype(jnp.bfloat16)
        strip[cut, length - rows : length] = jnp.where(kept, whole[:, length - rows :], 0.0).astype(
            jnp.bfloat16
        )


def strip_kernel(chips, rows, num, *refs):
    own = refs[:chips]
    pair = refs[chips : 2 * chips]
    taps_ref, signal, strip = refs[2 * chips :]
    length = 2 * chips * rows
    half = signal.shape[1] // 2
    wide = length + 2 * rows
    core = lax.axis_index("seq") % 2
    places = block_places(chips, range(chips))
    for own_block, pair_block, both in zip(own, pair, places, strict=True):
        for block, place in zip((own_block, pair_block), both, strict=True):
            value = block[...]
            turned = jnp.concatenate([value[:, half:], value[:, :half]], axis=1)
            value = jnp.where(core == 0, value, turned)
            signal[pl.ds(pl.multiple_of(place * rows, rows), rows), :] = value

    def one_filter(k, carry):
        line = jnp.broadcast_to(taps_ref[pl.ds(k, 1), :], (8, wide))
        line = pltpu.roll(line, wide - rows + 1, 1, stride=1, stride_axis=0)
        for step in range(rows // 16):
            pieces = [pltpu.roll(line, 16 * step + 8 * h, 1)[:, : length + rows] for h in (0, 1)]
            at = pl.multiple_of(k * rows + 16 * step, 16)
            strip[pl.ds(at, 16), :] = jnp.concatenate(pieces, axis=0).astype(jnp.bfloat16)
        return carry

    lax.fori_loop(0, num, one_filter, 0)


def branch_kernel(chips, rows, fine, kind, *refs):
    signal, strip, mix_ref, pair_mix_ref, out_ref, feats = refs
    index = lax.axis_index("seq")
    other, part = aim(index // 2, index % 2, kind)
    devices = 2 * chips
    num, half, width = mix_ref.shape
    offset = (devices - 1 - (2 * other + part)) * rows

    def convolve(steps):
        depth = 2 * rows * steps
        left = strip[:, pl.ds(pl.multiple_of(offset, rows), depth)]
        total = jnp.dot(left, signal[0:depth, :], preferred_element_type=jnp.float32)
        for k in range(num):
            for which in range(2):
                for g in range(rows // fine):
                    to = (which * num + k) * half
                    at = (2 * g + which) * half
                    feats[g * fine : (g + 1) * fine, to : to + half] = total[
                        k * fine : (k + 1) * fine, at : at + half
                    ].astype(jnp.bfloat16)

    for steps in range(1, chips + 1):
        pl.when(other == steps - 1)(functools.partial(convolve, steps))
    total = project(feats, mix_ref, pair_mix_ref)
    out_ref[...] = total.astype(out_ref.dtype)


def shifted_kernel(chips, rows, shift_ref, *refs):
    signal, strip, mix_ref, pair_mix_ref, out_ref, sums = refs
    index = lax.axis_index("seq")
    other = (index // 2) ^ shift_ref[0]
    devices = 2 * chips
    num, half, width = mix_ref.shape
    offset = (devices - 1 - (2 * other + index % 2)) * rows
    sums[...] = jnp.zeros(sums.shape, jnp.float32)

    def add_tokens(step, carry):
        at = pl.multiple_of(2 * rows * step, 2 * rows)
        left = strip[:, pl.ds(pl.multiple_of(offset + at, rows), 2 * rows)]
        sums[...] += jnp.dot(
            left, signal[pl.ds(at, 2 * rows), :], preferred_element_type=jnp.float32
        )
        return carry

    lax.fori_loop(0, other + 1, add_tokens, 0)
    total = jnp.zeros((rows, width), jnp.float32)
    for k in range(num):
        found = sums[k * rows : (k + 1) * rows, :].astype(jnp.bfloat16)
        weight = jnp.concatenate([mix_ref[k], pair_mix_ref[k]], axis=0)
        total += jnp.dot(found, weight, preferred_element_type=jnp.float32)
    out_ref[...] = total.astype(out_ref.dtype)


def local(tokens, norm_gain, filters, mixing):
    rows, width = tokens.shape
    devices = lax.axis_size("seq")
    chips = devices // 2
    num, span = filters.shape
    length = devices * rows
    count = width // chips
    relay = chips == 4 and count % 256 == 0 and span == rows and rows % EXTRA == 0 and num <= EXTRA
    pair_mixing = swap(mixing, 1, devices)
    fine = 32 if relay else rows
    flat = (EXTRA, rows // EXTRA * count + span) if relay else (rows, count)
    blocks = kernel_call(
        norm_kernel,
        "norm",
        [jax.ShapeDtypeStruct(flat, jnp.bfloat16)] * chips,
        [HBM] * 3,
        8 * MIB,
        [
            pltpu.VMEM((rows, width), tokens.dtype),
            pltpu.VMEM((1, width), norm_gain.dtype),
            pltpu.VMEM((num, span), filters.dtype),
            pltpu.SemaphoreType.DMA((3,)),
        ],
    )(in_hbm(tokens), in_hbm(norm_gain.reshape(1, width)), in_hbm(filters))
    near_mixing, first = kernel_call(
        stage_kernel,
        "stage",
        [
            jax.ShapeDtypeStruct(mixing.shape, mixing.dtype),
            jax.ShapeDtypeStruct(blocks[0].shape, blocks[0].dtype),
        ],
        [HBM, VMEM],
        8 * MIB,
        [pltpu.SemaphoreType.DMA(())],
    )(in_hbm(mixing), blocks[0])
    work = 2 * num * rows * count * (width + length)
    shifts = [0, 3, 1, 2] if relay else list(range(chips))
    own = {s: swap(blocks[s], 2 * s + 1, devices) for s in reversed(shifts) if s}
    own[0] = first
    pair = {s: swap(own[s], 1, devices) for s in shifts}
    own[0] = blocks[0]
    ends = [own[s] for s in shifts] + [pair[s] for s in shifts]
    shapes = [
        jax.ShapeDtypeStruct((length + rows, rows // fine * count), jnp.bfloat16),
        jax.ShapeDtypeStruct((num * fine, length + rows), jnp.bfloat16),
    ]
    if relay:
        signal, strip = kernel_call(
            functools.partial(merge_kernel, chips, shifts, rows, num, fine),
            "merge",
            shapes,
            [VMEM] * (2 * chips),
            16 * MIB,
            [pltpu.VMEM((EXTRA, length), jnp.float32)],
        )(*ends)
    else:
        taps = lax.all_gather(filters, "seq", axis=1, tiled=True)[:, ::-1]
        taps = jnp.pad(taps, ((0, EXTRA - num), (0, 2 * rows)))
        signal, strip = kernel_call(
            functools.partial(strip_kernel, chips, rows, num),
            "strip",
            shapes,
            [VMEM] * (2 * chips + 1),
            48 * MIB,
        )(*ends, taps)
    fixed = [signal, strip, near_mixing, pair_mixing]
    total = tokens.astype(jnp.float32)
    if relay:

        def branch(kind, dtype):
            return kernel_call(
                functools.partial(branch_kernel, chips, rows, fine, kind),
                "branch",
                jax.ShapeDtypeStruct((rows, width), dtype),
                [VMEM] * 4,
                24 * MIB,
                [pltpu.VMEM((rows, num * count), jnp.bfloat16)],
            )(*fixed)

        pairs = [(c, q) for c in range(chips) for q in range(2)]
        across = [(2 * c + q, 2 * (c ^ (1 + q)) + 1 - q) for c, q in pairs]
        along = [(2 * c + q, 2 * (c ^ (1 + q)) + q) for c, q in pairs]
        far = lax.ppermute(branch("far", jnp.bfloat16), "seq", across)
        early = lax.ppermute(branch("early", jnp.bfloat16), "seq", along)
        late = (branch("late", jnp.float32) + far.astype(jnp.float32)).astype(jnp.bfloat16)
        late = lax.ppermute(late, "seq", across)
        total = total + branch("own", jnp.float32)
        sent = [early, late]
    else:

        def branch(shift):
            return kernel_call(
                functools.partial(shifted_kernel, chips, rows),
                "branch",
                jax.ShapeDtypeStruct((rows, width), jnp.bfloat16),
                [SMEM] + [VMEM] * 4,
                48 * MIB,
                [pltpu.VMEM((num * rows, count), jnp.float32)],
            )(shift.reshape(1), *fixed)

        parts = lax.map(branch, jnp.arange(chips, dtype=jnp.int32))
        sent = [parts[0]] + [swap(parts[s], 2 * s, devices) for s in range(1, chips)]
    for value in sent:
        total = total + value.astype(jnp.float32)
    return total.astype(jnp.bfloat16)


def solution(mesh):
    in_specs = (P(("dp", "seq"), None), P(), P(None, "seq"), P(None, "seq", None))
    out_specs = P(("dp", "seq"), None)
    return jax.shard_map(local, mesh=mesh, in_specs=in_specs, out_specs=out_specs, check_vma=False)
```

```python
import functools

import jax
import jax.numpy as jnp
from jax import lax
from jax.experimental import pallas as pl
from jax.experimental.pallas import tpu as pltpu
from jax.sharding import PartitionSpec as P

MIB = 1024 * 1024
EXTRA = 16
GROUP = 6
VMEM = pl.BlockSpec(memory_space=pltpu.VMEM)
SMEM = pl.BlockSpec(memory_space=pltpu.SMEM)
HBM = pl.BlockSpec(memory_space=pltpu.HBM)


def swap(value, bits, size):
    return lax.ppermute(value, "seq", [(i, i ^ bits) for i in range(size)])


def kernel_call(kernel, name, out_shape, specs, limit, scratch=()):
    return pl.pallas_call(
        kernel,
        out_shape=out_shape,
        in_specs=specs,
        out_specs=jax.tree.map(lambda _: VMEM, out_shape),
        scratch_shapes=scratch,
        compiler_params=pltpu.CompilerParams(vmem_limit_bytes=limit),
        name=name,
    )


def in_hbm(value):
    return pltpu.with_memory_space_constraint(value, pltpu.HBM)


def norm_kernel(tokens_hbm, gain_hbm, filters_hbm, *refs):
    *out_refs, tokens_ref, gain_ref, filters_ref, sems = refs
    pairs = ((filters_hbm, filters_ref), (gain_hbm, gain_ref), (tokens_hbm, tokens_ref))
    copies = [pltpu.make_async_copy(a, b, sems.at[i]) for i, (a, b) in enumerate(pairs)]
    for copy in copies:
        copy.start()
    chip = lax.axis_index("seq") // 2
    rows, width = tokens_ref.shape
    chips = len(out_refs)
    count = width // chips
    num, span = filters_ref.shape
    packed = out_refs[0].shape[0] < rows
    copies[0].wait()
    if packed:
        flip = (
            lax.broadcasted_iota(jnp.int32, (span, span), 0)
            + lax.broadcasted_iota(jnp.int32, (span, span), 1)
            == span - 1
        ).astype(jnp.bfloat16)
        taps = jnp.dot(
            filters_ref[...].astype(jnp.bfloat16), flip, preferred_element_type=jnp.float32
        )
        taps = jnp.concatenate([taps, jnp.zeros((EXTRA - num, span), jnp.float32)], axis=0)
        for out_ref in out_refs:
            out_ref[:, rows // EXTRA * count :] = taps.astype(jnp.bfloat16)
    copies[1].wait()
    copies[2].wait()
    values = tokens_ref[...].astype(jnp.float32)
    scale = lax.rsqrt(jnp.mean(values * values, axis=1, keepdims=True) + 1e-05)
    normed = (values * scale * gain_ref[...]).astype(jnp.bfloat16)
    for part in range(chips):
        for shift, out_ref in enumerate(out_refs):

            @pl.when(chip == part ^ shift)
            def _(part=part, out_ref=out_ref):
                value = normed[:, part * count : (part + 1) * count]
                if not packed:
                    out_ref[...] = value
                    return
                for g in range(rows // EXTRA):
                    out_ref[:, g * count : (g + 1) * count] = value[g * EXTRA : (g + 1) * EXTRA]


def stage_kernel(mix_hbm, block_ref, mix_ref, out_ref, sem):
    copy = pltpu.make_async_copy(mix_hbm, mix_ref, sem)
    copy.start()
    out_ref[...] = block_ref[...]
    copy.wait()


def aim(chip, core, kind):
    if kind == "far":
        return chip ^ 3, core
    if kind == "own":
        return chip, core
    return chip ^ (1 + core), core if kind == "early" else 1 - core


def project(feats, mix_ref, pair_mix_ref):
    num, half, width = mix_ref.shape
    both = num * half
    return jnp.dot(
        feats[:, :both],
        mix_ref[...].reshape(both, width),
        preferred_element_type=jnp.float32,
    ) + jnp.dot(
        feats[:, both:],
        pair_mix_ref[...].reshape(both, width),
        preferred_element_type=jnp.float32,
    )


def block_places(chips, shifts):
    index = lax.axis_index("seq")
    chip = index // 2
    core = index % 2
    first = [core if s == 0 else 1 - core for s in shifts]
    return [(2 * (chip ^ s) + q, 2 * (chip ^ s) + 1 - q) for s, q in zip(shifts, first, strict=True)]


def ordered(value, core):
    half = value.shape[1] // 2
    turned = jnp.concatenate([value[:, half:], value[:, :half]], axis=1)
    return jnp.where(core == 0, value, turned)


def turn_taps(base, strip, k, fine, rows):
    length = base.shape[1]
    row = lax.broadcasted_iota(jnp.int32, (fine, rows), 0)
    lane = lax.broadcasted_iota(jnp.int32, (fine, rows), 1)
    kept = lane - row <= rows - fine
    line = jnp.broadcast_to(base[k : k + 1, :], (8, length))
    line = pltpu.roll(line, length - fine + 1, 1, stride=1, stride_axis=0)
    lines = [line] + [pltpu.roll(line, step, 1) for step in range(8, fine, 8)]
    whole = jnp.concatenate(lines, axis=0)
    cut = slice(k * fine, (k + 1) * fine)
    strip[cut, : length - rows] = whole[:, : length - rows].astype(jnp.bfloat16)
    strip[cut, length - rows : length] = jnp.where(kept, whole[:, length - rows :], 0.0).astype(
        jnp.bfloat16
    )


def write_features(feats, total, k, num, groups):
    fine = total.shape[0]
    half = total.shape[1] // groups // 2
    for which in range(2):
        for g in range(groups):
            to = (which * num + k) * half
            at = (2 * g + which) * half
            feats[g * fine : (g + 1) * fine, to : to + half] = total[:, at : at + half].astype(
                jnp.bfloat16
            )


def merge_kernel(chips, shifts, rows, num, fine, *refs):
    own = refs[:chips]
    pair = refs[chips : 2 * chips]
    mix_ref, pair_mix_ref, signal, strip, out_ref, base, feats = refs[2 * chips :]
    devices = 2 * chips
    length = devices * rows
    groups = rows // fine
    count = signal.shape[1] // groups
    core = lax.axis_index("seq") % 2
    late = [rows - fine * (g + 1) for g in range(groups)]
    for g in range(groups - 1):
        signal[0 : late[g], g * count : (g + 1) * count] = jnp.zeros((late[g], count), signal.dtype)
    places = block_places(chips, shifts)
    for own_block, pair_block, both in zip(own, pair, places, strict=True):
        for block, place in zip((own_block, pair_block), both, strict=True):
            for part in range(rows // EXTRA):
                value = ordered(block[:, part * count : (part + 1) * count], core)
                for g in range(groups):
                    at = pl.multiple_of(place * rows + late[g] + part * EXTRA, EXTRA)
                    signal[pl.ds(at, EXTRA), g * count : (g + 1) * count] = value
            at = pl.multiple_of((devices - 1 - place) * rows, rows)
            base[:, pl.ds(at, rows)] = block[:, rows // EXTRA * count :].astype(jnp.float32)
    strip[:, length:] = jnp.zeros((num * fine, rows), jnp.bfloat16)
    other, part = aim(lax.axis_index("seq") // 2, core, "far")
    offset = (devices - 1 - (2 * other + part)) * rows

    def convolve(steps):
        depth = 2 * rows * steps
        for first in range(0, num, GROUP):
            for k in range(first, first + GROUP):
                turn_taps(base, strip, k, fine, rows)
            left = strip[
                first * fine : (first + GROUP) * fine, pl.ds(pl.multiple_of(offset, rows), depth)
            ]
            total = jnp.dot(left, signal[0:depth, :], preferred_element_type=jnp.float32)
            for k in range(first, first + GROUP):
                write_features(feats, total[(k - first) * fine : (k - first + 1) * fine], k, num, groups)

    for steps in range(1, chips + 1):
        pl.when(other == steps - 1)(functools.partial(convolve, steps))
    total = project(feats, mix_ref, pair_mix_ref)
    out_ref[...] = total.astype(out_ref.dtype)


def strip_kernel(chips, rows, num, *refs):
    own = refs[:chips]
    pair = refs[chips : 2 * chips]
    taps_ref, signal, strip = refs[2 * chips :]
    length = 2 * chips * rows
    half = signal.shape[1] // 2
    wide = length + 2 * rows
    core = lax.axis_index("seq") % 2
    places = block_places(chips, range(chips))
    for own_block, pair_block, both in zip(own, pair, places, strict=True):
        for block, place in zip((own_block, pair_block), both, strict=True):
            value = block[...]
            turned = jnp.concatenate([value[:, half:], value[:, :half]], axis=1)
            value = jnp.where(core == 0, value, turned)
            signal[pl.ds(pl.multiple_of(place * rows, rows), rows), :] = value

    def one_filter(k, carry):
        line = jnp.broadcast_to(taps_ref[pl.ds(k, 1), :], (8, wide))
        line = pltpu.roll(line, wide - rows + 1, 1, stride=1, stride_axis=0)
        for step in range(rows // 16):
            pieces = [pltpu.roll(line, 16 * step + 8 * h, 1)[:, : length + rows] for h in (0, 1)]
            at = pl.multiple_of(k * rows + 16 * step, 16)
            strip[pl.ds(at, 16), :] = jnp.concatenate(pieces, axis=0).astype(jnp.bfloat16)
        return carry

    lax.fori_loop(0, num, one_filter, 0)


def branch_kernel(chips, rows, fine, kind, *refs):
    signal, strip, mix_ref, pair_mix_ref, out_ref, feats = refs
    index = lax.axis_index("seq")
    other, part = aim(index // 2, index % 2, kind)
    devices = 2 * chips
    num, half, width = mix_ref.shape
    offset = (devices - 1 - (2 * other + part)) * rows

    def convolve(steps):
        depth = 2 * rows * steps
        left = strip[:, pl.ds(pl.multiple_of(offset, rows), depth)]
        total = jnp.dot(left, signal[0:depth, :], preferred_element_type=jnp.float32)
        for k in range(num):
            write_features(feats, total[k * fine : (k + 1) * fine], k, num, rows // fine)

    for steps in range(1, chips + 1):
        pl.when(other == steps - 1)(functools.partial(convolve, steps))
    total = project(feats, mix_ref, pair_mix_ref)
    out_ref[...] = total.astype(out_ref.dtype)


def shifted_kernel(chips, rows, shift_ref, *refs):
    signal, strip, mix_ref, pair_mix_ref, out_ref, sums = refs
    index = lax.axis_index("seq")
    other = (index // 2) ^ shift_ref[0]
    devices = 2 * chips
    num, half, width = mix_ref.shape
    offset = (devices - 1 - (2 * other + index % 2)) * rows
    sums[...] = jnp.zeros(sums.shape, jnp.float32)

    def add_tokens(step, carry):
        at = pl.multiple_of(2 * rows * step, 2 * rows)
        left = strip[:, pl.ds(pl.multiple_of(offset + at, rows), 2 * rows)]
        sums[...] += jnp.dot(
            left, signal[pl.ds(at, 2 * rows), :], preferred_element_type=jnp.float32
        )
        return carry

    lax.fori_loop(0, other + 1, add_tokens, 0)
    total = jnp.zeros((rows, width), jnp.float32)
    for k in range(num):
        found = sums[k * rows : (k + 1) * rows, :].astype(jnp.bfloat16)
        weight = jnp.concatenate([mix_ref[k], pair_mix_ref[k]], axis=0)
        total += jnp.dot(found, weight, preferred_element_type=jnp.float32)
    out_ref[...] = total.astype(out_ref.dtype)


def local(tokens, norm_gain, filters, mixing):
    rows, width = tokens.shape
    devices = lax.axis_size("seq")
    chips = devices // 2
    num, span = filters.shape
    length = devices * rows
    count = width // chips
    relay = chips == 4 and count % 256 == 0 and span == rows and rows % EXTRA == 0 and num <= EXTRA and num % GROUP == 0
    pair_mixing = swap(mixing, 1, devices)
    fine = 32 if relay else rows
    flat = (EXTRA, rows // EXTRA * count + span) if relay else (rows, count)
    blocks = kernel_call(
        norm_kernel,
        "norm",
        [jax.ShapeDtypeStruct(flat, jnp.bfloat16)] * chips,
        [HBM] * 3,
        8 * MIB,
        [
            pltpu.VMEM((rows, width), tokens.dtype),
            pltpu.VMEM((1, width), norm_gain.dtype),
            pltpu.VMEM((num, span), filters.dtype),
            pltpu.SemaphoreType.DMA((3,)),
        ],
    )(in_hbm(tokens), in_hbm(norm_gain.reshape(1, width)), in_hbm(filters))
    near_mixing, first = kernel_call(
        stage_kernel,
        "stage",
        [
            jax.ShapeDtypeStruct(mixing.shape, mixing.dtype),
            jax.ShapeDtypeStruct(blocks[0].shape, blocks[0].dtype),
        ],
        [HBM, VMEM],
        8 * MIB,
        [pltpu.SemaphoreType.DMA(())],
    )(in_hbm(mixing), blocks[0])
    work = 2 * num * rows * count * (width + length)
    shifts = [0, 3, 1, 2] if relay else list(range(chips))
    own = {s: swap(blocks[s], 2 * s + 1, devices) for s in reversed(shifts) if s}
    own[0] = first
    pair = {s: swap(own[s], 1, devices) for s in shifts}
    own[0] = blocks[0]
    ends = [own[s] for s in shifts] + [pair[s] for s in shifts]
    shapes = [
        jax.ShapeDtypeStruct((length + rows, rows // fine * count), jnp.bfloat16),
        jax.ShapeDtypeStruct((num * fine, length + rows), jnp.bfloat16),
    ]
    if relay:
        block = jax.ShapeDtypeStruct((rows, width), jnp.bfloat16)
        signal, strip, far = kernel_call(
            functools.partial(merge_kernel, chips, shifts, rows, num, fine),
            "merge",
            [*shapes, block],
            [VMEM] * (2 * chips + 2),
            24 * MIB,
            [
                pltpu.VMEM((EXTRA, length), jnp.float32),
                pltpu.VMEM((rows, num * count), jnp.bfloat16),
            ],
        )(*ends, near_mixing, pair_mixing)
    else:
        taps = lax.all_gather(filters, "seq", axis=1, tiled=True)[:, ::-1]
        taps = jnp.pad(taps, ((0, EXTRA - num), (0, 2 * rows)))
        signal, strip = kernel_call(
            functools.partial(strip_kernel, chips, rows, num),
            "strip",
            shapes,
            [VMEM] * (2 * chips + 1),
            48 * MIB,
        )(*ends, taps)
    fixed = [signal, strip, near_mixing, pair_mixing]
    total = tokens.astype(jnp.float32)
    if relay:

        def branch(kind, dtype):
            return kernel_call(
                functools.partial(branch_kernel, chips, rows, fine, kind),
                "branch",
                jax.ShapeDtypeStruct((rows, width), dtype),
                [VMEM] * 4,
                24 * MIB,
                [pltpu.VMEM((rows, num * count), jnp.bfloat16)],
            )(*fixed)

        pairs = [(c, q) for c in range(chips) for q in range(2)]
        across = [(2 * c + q, 2 * (c ^ (1 + q)) + 1 - q) for c, q in pairs]
        along = [(2 * c + q, 2 * (c ^ (1 + q)) + q) for c, q in pairs]
        far = lax.ppermute(far, "seq", across)
        early = lax.ppermute(branch("early", jnp.bfloat16), "seq", along)
        late = (branch("late", jnp.float32) + far.astype(jnp.float32)).astype(jnp.bfloat16)
        late = lax.ppermute(late, "seq", across)
        total = total + branch("own", jnp.float32)
        sent = [early, late]
    else:

        def branch(shift):
            return kernel_call(
                functools.partial(shifted_kernel, chips, rows),
                "branch",
                jax.ShapeDtypeStruct((rows, width), jnp.bfloat16),
                [SMEM] + [VMEM] * 4,
                48 * MIB,
                [pltpu.VMEM((num * rows, count), jnp.float32)],
            )(shift.reshape(1), *fixed)

        parts = lax.map(branch, jnp.arange(chips, dtype=jnp.int32))
        sent = [parts[0]] + [swap(parts[s], 2 * s, devices) for s in range(1, chips)]
    for value in sent:
        total = total + value.astype(jnp.float32)
    return total.astype(jnp.bfloat16)


def solution(mesh):
    in_specs = (P(("dp", "seq"), None), P(), P(None, "seq"), P(None, "seq", None))
    out_specs = P(("dp", "seq"), None)
    return jax.shard_map(local, mesh=mesh, in_specs=in_specs, out_specs=out_specs, check_vma=False)
```

```python
import functools

import jax
import jax.numpy as jnp
from jax import lax
from jax.experimental import pallas as pl
from jax.experimental.pallas import tpu as pltpu
from jax.sharding import PartitionSpec as P

MIB = 1024 * 1024
EXTRA = 16
PARTS = 2
GROUP = 6
VMEM = pl.BlockSpec(memory_space=pltpu.VMEM)
SMEM = pl.BlockSpec(memory_space=pltpu.SMEM)
HBM = pl.BlockSpec(memory_space=pltpu.HBM)


def swap(value, bits, size):
    return lax.ppermute(value, "seq", [(i, i ^ bits) for i in range(size)])


def kernel_call(kernel, name, out_shape, specs, limit, scratch=()):
    return pl.pallas_call(
        kernel,
        out_shape=out_shape,
        in_specs=specs,
        out_specs=jax.tree.map(lambda _: VMEM, out_shape),
        scratch_shapes=scratch,
        compiler_params=pltpu.CompilerParams(vmem_limit_bytes=limit),
        name=name,
    )


def in_hbm(value):
    return pltpu.with_memory_space_constraint(value, pltpu.HBM)


def norm_kernel(tokens_hbm, gain_hbm, filters_hbm, *refs):
    *out_refs, tokens_ref, gain_ref, filters_ref, sems = refs
    pairs = ((filters_hbm, filters_ref), (gain_hbm, gain_ref), (tokens_hbm, tokens_ref))
    copies = [pltpu.make_async_copy(a, b, sems.at[i]) for i, (a, b) in enumerate(pairs)]
    for copy in copies:
        copy.start()
    chip = lax.axis_index("seq") // 2
    rows, width = tokens_ref.shape
    chips = len(out_refs)
    count = width // chips
    num, span = filters_ref.shape
    packed = out_refs[0].shape[0] < rows
    copies[0].wait()
    if packed:
        flip = (
            lax.broadcasted_iota(jnp.int32, (span, span), 0)
            + lax.broadcasted_iota(jnp.int32, (span, span), 1)
            == span - 1
        ).astype(jnp.bfloat16)
        taps = jnp.dot(
            filters_ref[...].astype(jnp.bfloat16), flip, preferred_element_type=jnp.float32
        )
        taps = jnp.concatenate([taps, jnp.zeros((EXTRA - num, span), jnp.float32)], axis=0)
        for out_ref in out_refs:
            out_ref[:, rows // EXTRA * count :] = taps.astype(jnp.bfloat16)
    copies[1].wait()
    copies[2].wait()
    values = tokens_ref[...].astype(jnp.float32)
    scale = lax.rsqrt(jnp.mean(values * values, axis=1, keepdims=True) + 1e-05)
    normed = (values * scale * gain_ref[...]).astype(jnp.bfloat16)
    for part in range(chips):
        for shift, out_ref in enumerate(out_refs):

            @pl.when(chip == part ^ shift)
            def _(part=part, out_ref=out_ref):
                value = normed[:, part * count : (part + 1) * count]
                if not packed:
                    out_ref[...] = value
                    return
                for g in range(rows // EXTRA):
                    out_ref[:, g * count : (g + 1) * count] = value[g * EXTRA : (g + 1) * EXTRA]


def stage_kernel(mix_hbm, block_ref, mix_ref, out_ref, sem):
    copy = pltpu.make_async_copy(mix_hbm, mix_ref, sem)
    copy.start()
    out_ref[...] = block_ref[...]
    copy.wait()


def finish_kernel(tokens_ref, own_ref, early_ref, late_ref, out_hbm, held, sems):
    chunk = held.shape[0] // PARTS
    copies = []
    for i in range(PARTS):
        cut = pl.ds(i * chunk, chunk)
        total = tokens_ref[cut, :].astype(jnp.float32) + own_ref[cut, :]
        total = total + early_ref[cut, :].astype(jnp.float32)
        held[cut, :] = (total + late_ref[cut, :].astype(jnp.float32)).astype(held.dtype)
        copies.append(pltpu.make_async_copy(held.at[cut], out_hbm.at[cut], sems.at[i]))
        copies[-1].start()
    for copy in copies:
        copy.wait()


def aim(chip, core, kind):
    if kind == "far":
        return chip ^ 3, core
    if kind == "own":
        return chip, core
    return chip ^ (2 - core), core if kind == "early" else 1 - core


def project(feats, mix_ref, pair_mix_ref):
    num, half, width = mix_ref.shape
    both = num * half
    return jnp.dot(
        feats[:, :both],
        mix_ref[...].reshape(both, width),
        preferred_element_type=jnp.float32,
    ) + jnp.dot(
        feats[:, both:],
        pair_mix_ref[...].reshape(both, width),
        preferred_element_type=jnp.float32,
    )


def block_places(chips, shifts):
    index = lax.axis_index("seq")
    chip = index // 2
    core = index % 2
    first = [core if s == 0 else 1 - core for s in shifts]
    return [(2 * (chip ^ s) + q, 2 * (chip ^ s) + 1 - q) for s, q in zip(shifts, first, strict=True)]


def ordered(value, core):
    half = value.shape[1] // 2
    turned = jnp.concatenate([value[:, half:], value[:, :half]], axis=1)
    return jnp.where(core == 0, value, turned)


def turn_taps(base, strip, k, fine, rows):
    length = base.shape[1]
    row = lax.broadcasted_iota(jnp.int32, (fine, rows), 0)
    lane = lax.broadcasted_iota(jnp.int32, (fine, rows), 1)
    kept = lane - row <= rows - fine
    line = jnp.broadcast_to(base[k : k + 1, :], (8, length))
    line = pltpu.roll(line, length - fine + 1, 1, stride=1, stride_axis=0)
    lines = [line] + [pltpu.roll(line, step, 1) for step in range(8, fine, 8)]
    whole = jnp.concatenate(lines, axis=0)
    cut = slice(k * fine, (k + 1) * fine)
    strip[cut, : length - rows] = whole[:, : length - rows].astype(jnp.bfloat16)
    strip[cut, length - rows : length] = jnp.where(kept, whole[:, length - rows :], 0.0).astype(
        jnp.bfloat16
    )


def write_features(feats, total, k, num, groups):
    fine = total.shape[0]
    half = total.shape[1] // groups // 2
    for which in range(2):
        for g in range(groups):
            to = (which * num + k) * half
            at = (2 * g + which) * half
            feats[g * fine : (g + 1) * fine, to : to + half] = total[:, at : at + half].astype(
                jnp.bfloat16
            )


def merge_kernel(chips, shifts, rows, num, fine, *refs):
    own = refs[:chips]
    pair = refs[chips : 2 * chips]
    mix_ref, pair_mix_ref, signal, strip, out_ref, base, feats = refs[2 * chips :]
    devices = 2 * chips
    length = devices * rows
    groups = rows // fine
    count = signal.shape[1] // groups
    core = lax.axis_index("seq") % 2
    late = [rows - fine * (g + 1) for g in range(groups)]
    for g in range(groups - 1):
        signal[0 : late[g], g * count : (g + 1) * count] = jnp.zeros((late[g], count), signal.dtype)
    places = block_places(chips, shifts)
    for own_block, pair_block, both in zip(own, pair, places, strict=True):
        for block, place in zip((own_block, pair_block), both, strict=True):
            for part in range(rows // EXTRA):
                value = ordered(block[:, part * count : (part + 1) * count], core)
                for g in range(groups):
                    at = pl.multiple_of(place * rows + late[g] + part * EXTRA, EXTRA)
                    signal[pl.ds(at, EXTRA), g * count : (g + 1) * count] = value
            at = pl.multiple_of((devices - 1 - place) * rows, rows)
            base[:, pl.ds(at, rows)] = block[:, rows // EXTRA * count :].astype(jnp.float32)
    strip[:, length:] = jnp.zeros((num * fine, rows), jnp.bfloat16)
    other, part = aim(lax.axis_index("seq") // 2, core, "far")
    offset = (devices - 1 - (2 * other + part)) * rows

    def convolve(steps):
        depth = 2 * rows * steps
        for first in range(0, num, GROUP):
            for k in range(first, first + GROUP):
                turn_taps(base, strip, k, fine, rows)
            left = strip[
                first * fine : (first + GROUP) * fine, pl.ds(pl.multiple_of(offset, rows), depth)
            ]
            total = jnp.dot(left, signal[0:depth, :], preferred_element_type=jnp.float32)
            for k in range(first, first + GROUP):
                write_features(feats, total[(k - first) * fine : (k - first + 1) * fine], k, num, groups)

    for steps in range(1, chips + 1):
        pl.when(other == steps - 1)(functools.partial(convolve, steps))
    total = project(feats, mix_ref, pair_mix_ref)
    out_ref[...] = total.astype(out_ref.dtype)


def strip_kernel(chips, rows, num, *refs):
    own = refs[:chips]
    pair = refs[chips : 2 * chips]
    taps_ref, signal, strip = refs[2 * chips :]
    length = 2 * chips * rows
    half = signal.shape[1] // 2
    wide = length + 2 * rows
    core = lax.axis_index("seq") % 2
    places = block_places(chips, range(chips))
    for own_block, pair_block, both in zip(own, pair, places, strict=True):
        for block, place in zip((own_block, pair_block), both, strict=True):
            value = block[...]
            turned = jnp.concatenate([value[:, half:], value[:, :half]], axis=1)
            value = jnp.where(core == 0, value, turned)
            signal[pl.ds(pl.multiple_of(place * rows, rows), rows), :] = value

    def one_filter(k, carry):
        line = jnp.broadcast_to(taps_ref[pl.ds(k, 1), :], (8, wide))
        line = pltpu.roll(line, wide - rows + 1, 1, stride=1, stride_axis=0)
        for step in range(rows // 16):
            pieces = [pltpu.roll(line, 16 * step + 8 * h, 1)[:, : length + rows] for h in (0, 1)]
            at = pl.multiple_of(k * rows + 16 * step, 16)
            strip[pl.ds(at, 16), :] = jnp.concatenate(pieces, axis=0).astype(jnp.bfloat16)
        return carry

    lax.fori_loop(0, num, one_filter, 0)


def branch_kernel(chips, rows, fine, kind, *refs):
    signal, strip, mix_ref, pair_mix_ref, out_ref, feats = refs
    index = lax.axis_index("seq")
    other, part = aim(index // 2, index % 2, kind)
    devices = 2 * chips
    num, half, width = mix_ref.shape
    offset = (devices - 1 - (2 * other + part)) * rows

    def convolve(steps):
        depth = 2 * rows * steps
        left = strip[:, pl.ds(pl.multiple_of(offset, rows), depth)]
        total = jnp.dot(left, signal[0:depth, :], preferred_element_type=jnp.float32)
        for k in range(num):
            write_features(feats, total[k * fine : (k + 1) * fine], k, num, rows // fine)

    for steps in range(1, chips + 1):
        pl.when(other == steps - 1)(functools.partial(convolve, steps))
    total = project(feats, mix_ref, pair_mix_ref)
    out_ref[...] = total.astype(out_ref.dtype)


def shifted_kernel(chips, rows, shift_ref, *refs):
    signal, strip, mix_ref, pair_mix_ref, out_ref, sums = refs
    index = lax.axis_index("seq")
    other = (index // 2) ^ shift_ref[0]
    devices = 2 * chips
    num, half, width = mix_ref.shape
    offset = (devices - 1 - (2 * other + index % 2)) * rows
    sums[...] = jnp.zeros(sums.shape, jnp.float32)

    def add_tokens(step, carry):
        at = pl.multiple_of(2 * rows * step, 2 * rows)
        left = strip[:, pl.ds(pl.multiple_of(offset + at, rows), 2 * rows)]
        sums[...] += jnp.dot(
            left, signal[pl.ds(at, 2 * rows), :], preferred_element_type=jnp.float32
        )
        return carry

    lax.fori_loop(0, other + 1, add_tokens, 0)
    total = jnp.zeros((rows, width), jnp.float32)
    for k in range(num):
        found = sums[k * rows : (k + 1) * rows, :].astype(jnp.bfloat16)
        weight = jnp.concatenate([mix_ref[k], pair_mix_ref[k]], axis=0)
        total += jnp.dot(found, weight, preferred_element_type=jnp.float32)
    out_ref[...] = total.astype(out_ref.dtype)


def local(tokens, norm_gain, filters, mixing):
    rows, width = tokens.shape
    devices = lax.axis_size("seq")
    chips = devices // 2
    num, span = filters.shape
    length = devices * rows
    count = width // chips
    relay = chips == 4 and count % 256 == 0 and span == rows and rows % EXTRA == 0 and num <= EXTRA and num % GROUP == 0
    pair_mixing = swap(mixing, 1, devices)
    fine = 32 if relay else rows
    flat = (EXTRA, rows // EXTRA * count + span) if relay else (rows, count)
    blocks = kernel_call(
        norm_kernel,
        "norm",
        [jax.ShapeDtypeStruct(flat, jnp.bfloat16)] * chips,
        [HBM] * 3,
        8 * MIB,
        [
            pltpu.VMEM((rows, width), tokens.dtype),
            pltpu.VMEM((1, width), norm_gain.dtype),
            pltpu.VMEM((num, span), filters.dtype),
            pltpu.SemaphoreType.DMA((3,)),
        ],
    )(in_hbm(tokens), in_hbm(norm_gain.reshape(1, width)), in_hbm(filters))
    near_mixing, first = kernel_call(
        stage_kernel,
        "stage",
        [
            jax.ShapeDtypeStruct(mixing.shape, mixing.dtype),
            jax.ShapeDtypeStruct(blocks[0].shape, blocks[0].dtype),
        ],
        [HBM, VMEM],
        8 * MIB,
        [pltpu.SemaphoreType.DMA(())],
    )(in_hbm(mixing), blocks[0])
    work = 2 * num * rows * count * (width + length)
    shifts = [0, 3, 2, 1] if relay else list(range(chips))
    own = {s: swap(blocks[s], 2 * s + 1, devices) for s in reversed(shifts) if s}
    own[0] = first
    pair = {s: swap(own[s], 1, devices) for s in shifts}
    own[0] = blocks[0]
    ends = [own[s] for s in shifts] + [pair[s] for s in shifts]
    shapes = [
        jax.ShapeDtypeStruct((length + rows, rows // fine * count), jnp.bfloat16),
        jax.ShapeDtypeStruct((num * fine, length + rows), jnp.bfloat16),
    ]
    if relay:
        block = jax.ShapeDtypeStruct((rows, width), jnp.bfloat16)
        signal, strip, far = kernel_call(
            functools.partial(merge_kernel, chips, shifts, rows, num, fine),
            "merge",
            [*shapes, block],
            [VMEM] * (2 * chips + 2),
            24 * MIB,
            [
                pltpu.VMEM((EXTRA, length), jnp.float32),
                pltpu.VMEM((rows, num * count), jnp.bfloat16),
            ],
        )(*ends, near_mixing, pair_mixing)
    else:
        taps = lax.all_gather(filters, "seq", axis=1, tiled=True)[:, ::-1]
        taps = jnp.pad(taps, ((0, EXTRA - num), (0, 2 * rows)))
        signal, strip = kernel_call(
            functools.partial(strip_kernel, chips, rows, num),
            "strip",
            shapes,
            [VMEM] * (2 * chips + 1),
            48 * MIB,
        )(*ends, taps)
    fixed = [signal, strip, near_mixing, pair_mixing]
    if relay:

        def branch(kind, dtype):
            return kernel_call(
                functools.partial(branch_kernel, chips, rows, fine, kind),
                "branch",
                jax.ShapeDtypeStruct((rows, width), dtype),
                [VMEM] * 4,
                24 * MIB,
                [pltpu.VMEM((rows, num * count), jnp.bfloat16)],
            )(*fixed)

        pairs = [(c, q) for c in range(chips) for q in range(2)]
        across = [(2 * c + q, 2 * (c ^ (2 - q)) + 1 - q) for c, q in pairs]
        along = [(2 * c + q, 2 * (c ^ (2 - q)) + q) for c, q in pairs]
        far = lax.ppermute(far, "seq", across)
        early = lax.ppermute(branch("early", jnp.bfloat16), "seq", along)
        late = (branch("late", jnp.float32) + far.astype(jnp.float32)).astype(jnp.bfloat16)
        late = lax.ppermute(late, "seq", across)
        return pl.pallas_call(
            finish_kernel,
            out_shape=jax.ShapeDtypeStruct((rows, width), tokens.dtype),
            in_specs=[VMEM] * 4,
            out_specs=HBM,
            scratch_shapes=[
                pltpu.VMEM((rows, width), tokens.dtype),
                pltpu.SemaphoreType.DMA((PARTS,)),
            ],
            compiler_params=pltpu.CompilerParams(vmem_limit_bytes=8 * MIB),
            name="finish",
        )(tokens, branch("own", jnp.float32), early, late)
    else:

        def branch(shift):
            return kernel_call(
                functools.partial(shifted_kernel, chips, rows),
                "branch",
                jax.ShapeDtypeStruct((rows, width), jnp.bfloat16),
                [SMEM] + [VMEM] * 4,
                48 * MIB,
                [pltpu.VMEM((num * rows, count), jnp.float32)],
            )(shift.reshape(1), *fixed)

        parts = lax.map(branch, jnp.arange(chips, dtype=jnp.int32))
        sent = [parts[0]] + [swap(parts[s], 2 * s, devices) for s in range(1, chips)]
    total = tokens.astype(jnp.float32)
    for value in sent:
        total = total + value.astype(jnp.float32)
    return total.astype(jnp.bfloat16)


def solution(mesh):
    in_specs = (P(("dp", "seq"), None), P(), P(None, "seq"), P(None, "seq", None))
    out_specs = P(("dp", "seq"), None)
    return jax.shard_map(local, mesh=mesh, in_specs=in_specs, out_specs=out_specs, check_vma=False)
```

```python
import functools

import jax
import jax.numpy as jnp
from jax import lax
from jax.experimental import pallas as pl
from jax.experimental.pallas import tpu as pltpu
from jax.sharding import PartitionSpec as P

MIB = 1024 * 1024
EXTRA = 16
PARTS = 2
GROUP = 6
VMEM = pl.BlockSpec(memory_space=pltpu.VMEM)
SMEM = pl.BlockSpec(memory_space=pltpu.SMEM)
HBM = pl.BlockSpec(memory_space=pltpu.HBM)


def swap(value, bits, size):
    return lax.ppermute(value, "seq", [(i, i ^ bits) for i in range(size)])


def kernel_call(kernel, name, out_shape, specs, limit, scratch=()):
    return pl.pallas_call(
        kernel,
        out_shape=out_shape,
        in_specs=specs,
        out_specs=jax.tree.map(lambda _: VMEM, out_shape),
        scratch_shapes=scratch,
        compiler_params=pltpu.CompilerParams(vmem_limit_bytes=limit),
        name=name,
    )


def in_hbm(value):
    return pltpu.with_memory_space_constraint(value, pltpu.HBM)


def norm_kernel(tokens_hbm, gain_hbm, filters_hbm, *refs):
    *out_refs, tokens_ref, gain_ref, filters_ref, sems = refs
    pairs = ((filters_hbm, filters_ref), (gain_hbm, gain_ref), (tokens_hbm, tokens_ref))
    copies = [pltpu.make_async_copy(a, b, sems.at[i]) for i, (a, b) in enumerate(pairs)]
    for copy in copies:
        copy.start()
    chip = lax.axis_index("seq") // 2
    rows, width = tokens_ref.shape
    chips = len(out_refs)
    count = width // chips
    num, span = filters_ref.shape
    packed = out_refs[0].shape[0] < rows
    copies[0].wait()
    if packed:
        flip = (
            lax.broadcasted_iota(jnp.int32, (span, span), 0)
            + lax.broadcasted_iota(jnp.int32, (span, span), 1)
            == span - 1
        ).astype(jnp.bfloat16)
        taps = jnp.dot(
            filters_ref[...].astype(jnp.bfloat16), flip, preferred_element_type=jnp.float32
        )
        taps = jnp.concatenate([taps, jnp.zeros((EXTRA - num, span), jnp.float32)], axis=0)
        for out_ref in out_refs:
            out_ref[:, rows // EXTRA * count :] = taps.astype(jnp.bfloat16)
    copies[1].wait()
    copies[2].wait()
    values = tokens_ref[...].astype(jnp.float32)
    scale = lax.rsqrt(jnp.mean(values * values, axis=1, keepdims=True) + 1e-05)
    normed = (values * scale * gain_ref[...]).astype(jnp.bfloat16)
    for part in range(chips):
        for shift, out_ref in enumerate(out_refs):

            @pl.when(chip == part ^ shift)
            def _(part=part, out_ref=out_ref):
                value = normed[:, part * count : (part + 1) * count]
                if not packed:
                    out_ref[...] = value
                    return
                for g in range(rows // EXTRA):
                    out_ref[:, g * count : (g + 1) * count] = value[g * EXTRA : (g + 1) * EXTRA]


def stage_kernel(mix_hbm, block_ref, mix_ref, out_ref, sem):
    copy = pltpu.make_async_copy(mix_hbm, mix_ref, sem)
    copy.start()
    out_ref[...] = block_ref[...]
    copy.wait()


def finish_kernel(own_ref, late_ref, out_hbm, held, sems):
    chunk = held.shape[0] // PARTS
    copies = []
    for i in range(PARTS):
        cut = pl.ds(i * chunk, chunk)
        held[cut, :] = (own_ref[cut, :] + late_ref[cut, :].astype(jnp.float32)).astype(held.dtype)
        copies.append(pltpu.make_async_copy(held.at[cut], out_hbm.at[cut], sems.at[i]))
        copies[-1].start()
    for copy in copies:
        copy.wait()


def aim(chip, core, kind):
    if kind == "far":
        return chip ^ 3, core
    if kind == "own":
        return chip, core
    return chip ^ (2 - core), core if kind == "early" else 1 - core


def project(feats, mix_ref, pair_mix_ref):
    num, half, width = mix_ref.shape
    both = num * half
    return jnp.dot(
        feats[:, :both],
        mix_ref[...].reshape(both, width),
        preferred_element_type=jnp.float32,
    ) + jnp.dot(
        feats[:, both:],
        pair_mix_ref[...].reshape(both, width),
        preferred_element_type=jnp.float32,
    )


def block_places(chips, shifts):
    index = lax.axis_index("seq")
    chip = index // 2
    core = index % 2
    first = [core if s == 0 else 1 - core for s in shifts]
    return [(2 * (chip ^ s) + q, 2 * (chip ^ s) + 1 - q) for s, q in zip(shifts, first, strict=True)]


def ordered(value, core):
    half = value.shape[1] // 2
    turned = jnp.concatenate([value[:, half:], value[:, :half]], axis=1)
    return jnp.where(core == 0, value, turned)


def turn_taps(base, strip, k, fine, rows):
    length = base.shape[1]
    row = lax.broadcasted_iota(jnp.int32, (fine, rows), 0)
    lane = lax.broadcasted_iota(jnp.int32, (fine, rows), 1)
    kept = lane - row <= rows - fine
    line = jnp.broadcast_to(base[k : k + 1, :], (8, length))
    line = pltpu.roll(line, length - fine + 1, 1, stride=1, stride_axis=0)
    lines = [line] + [pltpu.roll(line, step, 1) for step in range(8, fine, 8)]
    whole = jnp.concatenate(lines, axis=0)
    cut = slice(k * fine, (k + 1) * fine)
    strip[cut, : length - rows] = whole[:, : length - rows].astype(jnp.bfloat16)
    strip[cut, length - rows : length] = jnp.where(kept, whole[:, length - rows :], 0.0).astype(
        jnp.bfloat16
    )


def write_features(feats, total, k, num, groups):
    fine = total.shape[0]
    half = total.shape[1] // groups // 2
    for which in range(2):
        for g in range(groups):
            to = (which * num + k) * half
            at = (2 * g + which) * half
            feats[g * fine : (g + 1) * fine, to : to + half] = total[:, at : at + half].astype(
                jnp.bfloat16
            )


def merge_kernel(chips, shifts, rows, num, fine, *refs):
    own = refs[:chips]
    pair = refs[chips : 2 * chips]
    mix_ref, pair_mix_ref, signal, strip, out_ref, base, feats = refs[2 * chips :]
    devices = 2 * chips
    length = devices * rows
    groups = rows // fine
    count = signal.shape[1] // groups
    core = lax.axis_index("seq") % 2
    late = [rows - fine * (g + 1) for g in range(groups)]
    for g in range(groups - 1):
        signal[0 : late[g], g * count : (g + 1) * count] = jnp.zeros((late[g], count), signal.dtype)
    places = block_places(chips, shifts)
    for own_block, pair_block, both in zip(own, pair, places, strict=True):
        for block, place in zip((own_block, pair_block), both, strict=True):
            for part in range(rows // EXTRA):
                value = ordered(block[:, part * count : (part + 1) * count], core)
                for g in range(groups):
                    at = pl.multiple_of(place * rows + late[g] + part * EXTRA, EXTRA)
                    signal[pl.ds(at, EXTRA), g * count : (g + 1) * count] = value
            at = pl.multiple_of((devices - 1 - place) * rows, rows)
            base[:, pl.ds(at, rows)] = block[:, rows // EXTRA * count :].astype(jnp.float32)
    strip[:, length:] = jnp.zeros((num * fine, rows), jnp.bfloat16)
    other, part = aim(lax.axis_index("seq") // 2, core, "far")
    offset = (devices - 1 - (2 * other + part)) * rows

    def convolve(steps):
        depth = 2 * rows * steps
        for first in range(0, num, GROUP):
            for k in range(first, first + GROUP):
                turn_taps(base, strip, k, fine, rows)
            left = strip[
                first * fine : (first + GROUP) * fine, pl.ds(pl.multiple_of(offset, rows), depth)
            ]
            total = jnp.dot(left, signal[0:depth, :], preferred_element_type=jnp.float32)
            for k in range(first, first + GROUP):
                write_features(feats, total[(k - first) * fine : (k - first + 1) * fine], k, num, groups)

    for steps in range(1, chips + 1):
        pl.when(other == steps - 1)(functools.partial(convolve, steps))
    total = project(feats, mix_ref, pair_mix_ref)
    out_ref[...] = total.astype(out_ref.dtype)


def strip_kernel(chips, rows, num, *refs):
    own = refs[:chips]
    pair = refs[chips : 2 * chips]
    taps_ref, signal, strip = refs[2 * chips :]
    length = 2 * chips * rows
    half = signal.shape[1] // 2
    wide = length + 2 * rows
    core = lax.axis_index("seq") % 2
    places = block_places(chips, range(chips))
    for own_block, pair_block, both in zip(own, pair, places, strict=True):
        for block, place in zip((own_block, pair_block), both, strict=True):
            value = block[...]
            turned = jnp.concatenate([value[:, half:], value[:, :half]], axis=1)
            value = jnp.where(core == 0, value, turned)
            signal[pl.ds(pl.multiple_of(place * rows, rows), rows), :] = value

    def one_filter(k, carry):
        line = jnp.broadcast_to(taps_ref[pl.ds(k, 1), :], (8, wide))
        line = pltpu.roll(line, wide - rows + 1, 1, stride=1, stride_axis=0)
        for step in range(rows // 16):
            pieces = [pltpu.roll(line, 16 * step + 8 * h, 1)[:, : length + rows] for h in (0, 1)]
            at = pl.multiple_of(k * rows + 16 * step, 16)
            strip[pl.ds(at, 16), :] = jnp.concatenate(pieces, axis=0).astype(jnp.bfloat16)
        return carry

    lax.fori_loop(0, num, one_filter, 0)


def branch_kernel(chips, rows, fine, kind, *refs):
    signal, strip, mix_ref, pair_mix_ref, *more, out_ref, feats = refs
    index = lax.axis_index("seq")
    other, part = aim(index // 2, index % 2, kind)
    devices = 2 * chips
    num, half, width = mix_ref.shape
    offset = (devices - 1 - (2 * other + part)) * rows

    def convolve(steps):
        depth = 2 * rows * steps
        left = strip[:, pl.ds(pl.multiple_of(offset, rows), depth)]
        total = jnp.dot(left, signal[0:depth, :], preferred_element_type=jnp.float32)
        for k in range(num):
            write_features(feats, total[k * fine : (k + 1) * fine], k, num, rows // fine)

    for steps in range(1, chips + 1):
        pl.when(other == steps - 1)(functools.partial(convolve, steps))
    total = project(feats, mix_ref, pair_mix_ref)
    for ref in more:
        total = total + ref[...].astype(jnp.float32)
    out_ref[...] = total.astype(out_ref.dtype)


def shifted_kernel(chips, rows, shift_ref, *refs):
    signal, strip, mix_ref, pair_mix_ref, out_ref, sums = refs
    index = lax.axis_index("seq")
    other = (index // 2) ^ shift_ref[0]
    devices = 2 * chips
    num, half, width = mix_ref.shape
    offset = (devices - 1 - (2 * other + index % 2)) * rows
    sums[...] = jnp.zeros(sums.shape, jnp.float32)

    def add_tokens(step, carry):
        at = pl.multiple_of(2 * rows * step, 2 * rows)
        left = strip[:, pl.ds(pl.multiple_of(offset + at, rows), 2 * rows)]
        sums[...] += jnp.dot(
            left, signal[pl.ds(at, 2 * rows), :], preferred_element_type=jnp.float32
        )
        return carry

    lax.fori_loop(0, other + 1, add_tokens, 0)
    total = jnp.zeros((rows, width), jnp.float32)
    for k in range(num):
        found = sums[k * rows : (k + 1) * rows, :].astype(jnp.bfloat16)
        weight = jnp.concatenate([mix_ref[k], pair_mix_ref[k]], axis=0)
        total += jnp.dot(found, weight, preferred_element_type=jnp.float32)
    out_ref[...] = total.astype(out_ref.dtype)


def local(tokens, norm_gain, filters, mixing):
    rows, width = tokens.shape
    devices = lax.axis_size("seq")
    chips = devices // 2
    num, span = filters.shape
    length = devices * rows
    count = width // chips
    relay = chips == 4 and count % 256 == 0 and span == rows and rows % EXTRA == 0 and num <= EXTRA and num % GROUP == 0
    pair_mixing = swap(mixing, 1, devices)
    fine = 32 if relay else rows
    flat = (EXTRA, rows // EXTRA * count + span) if relay else (rows, count)
    blocks = kernel_call(
        norm_kernel,
        "norm",
        [jax.ShapeDtypeStruct(flat, jnp.bfloat16)] * chips,
        [HBM] * 3,
        8 * MIB,
        [
            pltpu.VMEM((rows, width), tokens.dtype),
            pltpu.VMEM((1, width), norm_gain.dtype),
            pltpu.VMEM((num, span), filters.dtype),
            pltpu.SemaphoreType.DMA((3,)),
        ],
    )(in_hbm(tokens), in_hbm(norm_gain.reshape(1, width)), in_hbm(filters))
    near_mixing, first = kernel_call(
        stage_kernel,
        "stage",
        [
            jax.ShapeDtypeStruct(mixing.shape, mixing.dtype),
            jax.ShapeDtypeStruct(blocks[0].shape, blocks[0].dtype),
        ],
        [HBM, VMEM],
        8 * MIB,
        [pltpu.SemaphoreType.DMA(())],
    )(in_hbm(mixing), blocks[0])
    work = 2 * num * rows * count * (width + length)
    shifts = [0, 3, 2, 1] if relay else list(range(chips))
    own = {s: swap(blocks[s], 2 * s + 1, devices) for s in reversed(shifts) if s}
    own[0] = first
    pair = {s: swap(own[s], 1, devices) for s in shifts}
    own[0] = blocks[0]
    ends = [own[s] for s in shifts] + [pair[s] for s in shifts]
    shapes = [
        jax.ShapeDtypeStruct((length + rows, rows // fine * count), jnp.bfloat16),
        jax.ShapeDtypeStruct((num * fine, length + rows), jnp.bfloat16),
    ]
    if relay:
        block = jax.ShapeDtypeStruct((rows, width), jnp.bfloat16)
        signal, strip, far = kernel_call(
            functools.partial(merge_kernel, chips, shifts, rows, num, fine),
            "merge",
            [*shapes, block],
            [VMEM] * (2 * chips + 2),
            24 * MIB,
            [
                pltpu.VMEM((EXTRA, length), jnp.float32),
                pltpu.VMEM((rows, num * count), jnp.bfloat16),
            ],
        )(*ends, near_mixing, pair_mixing)
    else:
        taps = lax.all_gather(filters, "seq", axis=1, tiled=True)[:, ::-1]
        taps = jnp.pad(taps, ((0, EXTRA - num), (0, 2 * rows)))
        signal, strip = kernel_call(
            functools.partial(strip_kernel, chips, rows, num),
            "strip",
            shapes,
            [VMEM] * (2 * chips + 1),
            48 * MIB,
        )(*ends, taps)
    fixed = [signal, strip, near_mixing, pair_mixing]
    if relay:

        def branch(kind, dtype, *more):
            return kernel_call(
                functools.partial(branch_kernel, chips, rows, fine, kind),
                "branch",
                jax.ShapeDtypeStruct((rows, width), dtype),
                [VMEM] * (4 + len(more)),
                24 * MIB,
                [pltpu.VMEM((rows, num * count), jnp.bfloat16)],
            )(*fixed, *more)

        pairs = [(c, q) for c in range(chips) for q in range(2)]
        across = [(2 * c + q, 2 * (c ^ (2 - q)) + 1 - q) for c, q in pairs]
        along = [(2 * c + q, 2 * (c ^ (2 - q)) + q) for c, q in pairs]
        far = lax.ppermute(far, "seq", across)
        early = lax.ppermute(branch("early", jnp.bfloat16), "seq", along)
        late = (branch("late", jnp.float32) + far.astype(jnp.float32)).astype(jnp.bfloat16)
        late = lax.ppermute(late, "seq", across)
        return pl.pallas_call(
            finish_kernel,
            out_shape=jax.ShapeDtypeStruct((rows, width), tokens.dtype),
            in_specs=[VMEM] * 2,
            out_specs=HBM,
            scratch_shapes=[
                pltpu.VMEM((rows, width), tokens.dtype),
                pltpu.SemaphoreType.DMA((PARTS,)),
            ],
            compiler_params=pltpu.CompilerParams(vmem_limit_bytes=8 * MIB),
            name="finish",
        )(branch("own", jnp.float32, tokens, early), late)
    else:

        def branch(shift):
            return kernel_call(
                functools.partial(shifted_kernel, chips, rows),
                "branch",
                jax.ShapeDtypeStruct((rows, width), jnp.bfloat16),
                [SMEM] + [VMEM] * 4,
                48 * MIB,
                [pltpu.VMEM((num * rows, count), jnp.float32)],
            )(shift.reshape(1), *fixed)

        parts = lax.map(branch, jnp.arange(chips, dtype=jnp.int32))
        sent = [parts[0]] + [swap(parts[s], 2 * s, devices) for s in range(1, chips)]
    total = tokens.astype(jnp.float32)
    for value in sent:
        total = total + value.astype(jnp.float32)
    return total.astype(jnp.bfloat16)


def solution(mesh):
    in_specs = (P(("dp", "seq"), None), P(), P(None, "seq"), P(None, "seq", None))
    out_specs = P(("dp", "seq"), None)
    return jax.shard_map(local, mesh=mesh, in_specs=in_specs, out_specs=out_specs, check_vma=False)
```
